128 devices in a mesh: dp: 8 (over x_lo, z), shard: 16 (over y, x_hi, core).
Axes of the slice: x: 4 (x_hi: 2, x_lo: 2; x = x_hi * 2 + x_lo), y: 4, z: 4, core: 2. Of those that a mesh axis runs over, the one named last changes fastest.
Arguments:
- states: bfloat16 [110592, 5120], P(('dp', 'shard')), may hold values from -6 to 6
- readout: bfloat16 [110592, 512], P(('dp', 'shard')), may hold values from -0.119628906 to 0.119628906
- logp_shift: bfloat16 [110592], P(('dp', 'shard')), may hold values from -0.59765625 to 0.59765625
- advantage: bfloat16 [110592], P(('dp', 'shard')), may hold values from -6 to 6
- response_mask: int32 [110592], P(('dp', 'shard')), may hold values 0 or 1
- rollout_len: int32 [128], P(('dp', 'shard')), may hold values from 144 to 864, as said below
- dest_slot: int32 [110592], P(('dp', 'shard')), may hold values from -1 to 4607, as said below
- weight: float32 [5120, 512], P('shard'), may hold values from -0.078125 to 0.078125
- moment1: float32 [5120, 512], P('shard'), may hold values from -0.0006 to 0.0006
- moment2: float32 [5120, 512], P('shard'), may hold values from 1e-09 to 1e-07
Outputs:
- weight_out: float32 [5120, 512], P('shard')
- moment1_out: float32 [5120, 512], P('shard')
- moment2_out: float32 [5120, 512], P('shard')
The draws below stay inside these ranges and needn't reach their ends.
Inputs may be any that keep to these rules, and one draw needn't show every extreme that they name: `rollout_len`: in each group of devices with one shard index, one device holds 864 live rows and the others between 144 and 288. `dest_slot`: live rows name distinct (dp index, slot) pairs within a group of devices with one shard index; at most 864 // 8 rows of one device name one dp index, and in each group one device sends exactly that many to every dp index.
All inputs are finite; a program needn't handle non-finite values. No bound on the sum of `response_mask` on one device may be relied on, other than what follows from the above.
Results may differ from the reference program's by a relative error of at most 0.0045.
Values may be sent and summed in bfloat16 or wider, within the bound.
A program may use at most 128 MiB of HBM per device.

```python
import math
import jax
import jax.numpy as jnp
from jax import lax

D = 5120
VW = 512
BAL = 576
UPDATES = 2
PRIOR_STEPS = 100
ROWS_IN = 864
MB = 288
N_DP = 8
N_SHARD = 16
DEVICES = 128


def balance_plan(key):
    key = jax.random.fold_in(key, 11)
    key_base, key_heavy = jax.random.split(key)
    groups = N_DP
    shards = N_SHARD
    base_len = jax.random.randint(key_base, (groups, shards), BAL // 4, BAL // 2 + 1)
    heavy_idx = jax.random.randint(key_heavy, (shards,), 0, groups)
    lengths = jnp.where(jnp.arange(groups)[:, None] == heavy_idx[None, :], ROWS_IN, base_len).astype(jnp.int32)
    live_rows = (jnp.arange(ROWS_IN)[None, None, :] < lengths[:, :, None]).astype(jnp.int32)
    by_shard = jnp.transpose(live_rows, (1, 0, 2)).reshape(shards, groups * ROWS_IN)
    row_rank = jnp.cumsum(by_shard, axis=1) - by_shard
    target = row_rank % groups
    turn_idx = row_rank // groups
    position = BAL - 1 - (turn_idx % UPDATES * (BAL // UPDATES) + turn_idx // UPDATES)
    dest_all = jnp.where(by_shard > 0, target * BAL + position, -1)
    dest_all = jnp.transpose(dest_all.reshape(shards, groups, ROWS_IN), (1, 0, 2)).reshape(-1)
    return (lengths.reshape(-1), dest_all.astype(jnp.int32))


def draw_rollout_len(key, part):
    return balance_plan(key)[0]


def draw_dest_slot(key, part):
    return balance_plan(key)[1]


def with_ends(result, stream_key, least, high):
    dims = result.shape
    place = [jax.random.randint(jax.random.fold_in(stream_key, axis), (), 0, dims[axis]) for axis in range(len(dims))]
    result = result.at[tuple(place)].set(least)
    longest = dims.index(max(dims))
    place[longest] = (place[longest] + 1) % dims[longest]
    return result.at[tuple(place)].set(high)


def level_of(stream_key, extent, pieces, smallest, high):
    level, own = 1.0, jax.random.fold_in(stream_key, 6)
    for dim, blocks in pieces:
        heights = jnp.exp(jax.random.uniform(jax.random.fold_in(own, dim), (blocks,), jnp.float32, smallest / len(pieces), high / len(pieces)))
        level = level * jnp.repeat(heights, extent[dim] // blocks).reshape([-1 if axis == dim else 1 for axis in range(len(extent))])
    return level


def centred(stream_key, dims, width, limit, cuts=(), held_as=jnp.bfloat16):
    result = width * jax.random.normal(stream_key, dims, jnp.float32)
    if cuts:
        result = result * level_of(stream_key, dims, cuts, -0.22, 0.18)
    return jnp.clip(result, -limit, limit).astype(held_as)


def setup_inputs(seed: int = 0) -> dict:
    streams_of = jax.random.split(jax.random.key(seed), 11)
    return {
        "states": centred(streams_of[0], (DEVICES * ROWS_IN, D), 1.0, 6.0, ((0, 128),)),
        "readout": centred(streams_of[1], (DEVICES * ROWS_IN, VW), 0.02, 0.119628906, ((0, 128),)),
        "logp_shift": centred(streams_of[2], (DEVICES * ROWS_IN,), 0.1, 0.59765625, ((0, 128),)),
        "advantage": centred(streams_of[3], (DEVICES * ROWS_IN,), 1.0, 6.0, ((0, 128),)),
        "response_mask": with_ends((jax.random.randint(streams_of[4], (DEVICES * ROWS_IN,), 0, 4) < 3).astype(jnp.int32), jax.random.fold_in(streams_of[4], 1), 0, 1),
        "rollout_len": draw_rollout_len(jax.random.fold_in(streams_of[10], 71), 0),
        "dest_slot": draw_dest_slot(jax.random.fold_in(streams_of[10], 71), 0),
        "weight": centred(streams_of[7], (D, VW), D ** -0.5, 0.078125, ((0, 16),), jnp.float32),
        "moment1": centred(streams_of[8], (D, VW), 0.0001, 0.0006, ((0, 16),), jnp.float32),
        "moment2": jnp.clip(jnp.exp(math.log(1.0000000116860974e-07) - 4.6051702 * jax.random.uniform(streams_of[9], (D, VW), jnp.float32) ** level_of(streams_of[9], (D, VW), ((0, 16),), -0.2, 0.2)), 9.999999717180685e-10, 1.0000000116860974e-07),
    }


BETA_ONE = 0.9
BETA_TWO = 0.999
LEARN_RATE = 0.001
DECAY_RATE = 0.01
ADAM_EPS = 1e-08
CLIP_EPS = 0.2

def surrogate_coeff(log_ratio, adv_rows, weights, token_total):
    prob_ratio = jnp.exp(log_ratio)
    clipped = jnp.clip(prob_ratio, 1.0 - CLIP_EPS, 1.0 + CLIP_EPS)
    chosen = (prob_ratio * adv_rows <= clipped * adv_rows).astype(jnp.float32)
    return -(weights / token_total) * adv_rows * prob_ratio * chosen

def adam_step(master, moment_one, moment_two, gradient, step_num):
    moment_one = BETA_ONE * moment_one + (1.0 - BETA_ONE) * gradient
    moment_two = BETA_TWO * moment_two + (1.0 - BETA_TWO) * gradient * gradient
    first_hat = moment_one / (1.0 - BETA_ONE ** step_num)
    second_hat = moment_two / (1.0 - BETA_TWO ** step_num)
    master = master - LEARN_RATE * (first_hat / (jnp.sqrt(second_hat) + ADAM_EPS) + DECAY_RATE * master)
    return (master, moment_one, moment_two)

def batch_of(values_all, devices, update):
    shaped = values_all.reshape((devices, BAL) + values_all.shape[1:])
    window = shaped[:, update * MB:(update + 1) * MB]
    return window.reshape((devices * MB,) + values_all.shape[1:])

def reference(states, readout, logp_shift, advantage, response_mask, rollout_len, dest_slot, weight, moment1, moment2):
    devices = N_DP * N_SHARD
    row_index = jnp.arange(devices * ROWS_IN, dtype=jnp.int32)
    device_of = (row_index // ROWS_IN).astype(jnp.int32)
    local_row = (row_index % ROWS_IN).astype(jnp.int32)
    live_rows = (local_row < rollout_len[device_of]) & (dest_slot >= 0)
    owner_idx = jnp.where(live_rows, dest_slot // BAL, 0)
    target = (owner_idx * N_SHARD + device_of % N_SHARD) * BAL + dest_slot % BAL
    target = jnp.where(live_rows, target, devices * BAL).astype(jnp.int32)
    bal_states = jnp.zeros((devices * BAL, D), jnp.bfloat16).at[target].set(states, mode='drop')
    bal_read = jnp.zeros((devices * BAL, VW), jnp.bfloat16).at[target].set(readout, mode='drop')
    bal_shift = jnp.zeros((devices * BAL,), jnp.float32).at[target].set(logp_shift.astype(jnp.float32), mode='drop')
    bal_adv = jnp.zeros((devices * BAL,), jnp.float32).at[target].set(advantage.astype(jnp.float32), mode='drop')
    bal_weight = jnp.zeros((devices * BAL,), jnp.float32).at[target].set(response_mask.astype(jnp.float32), mode='drop')
    master, moment_one, moment_two = (weight, moment1, moment2)
    for update in range(UPDATES):
        batch_states = batch_of(bal_states, devices, update)
        batch_read = batch_of(bal_read, devices, update)
        batch_shift = batch_of(bal_shift, devices, update)
        batch_adv = batch_of(bal_adv, devices, update)
        batch_weight = batch_of(bal_weight, devices, update)
        token_total = jnp.maximum(jnp.sum(batch_weight), 1.0)
        projected = jnp.dot(batch_states, master.astype(jnp.bfloat16), preferred_element_type=jnp.float32)
        log_ratio = batch_shift + lax.optimization_barrier(jnp.sum(projected * batch_read.astype(jnp.float32), axis=1))
        coefficient = surrogate_coeff(log_ratio, batch_adv, batch_weight, token_total)
        scaled = (coefficient[:, None] * batch_read.astype(jnp.float32)).astype(jnp.bfloat16)
        gradient = jnp.dot(batch_states.T, scaled, preferred_element_type=jnp.float32)
        master, moment_one, moment_two = adam_step(master, moment_one, moment_two, gradient, PRIOR_STEPS + update + 1)
    return (master, moment_one, moment_two)
```

```python
import jax
import jax.numpy as jnp
from jax import lax
from jax.experimental import pallas as pl
from jax.experimental.pallas import tpu as pltpu
from jax.sharding import PartitionSpec as P

MESH = pl.DeviceIdType.MESH

BAL = 576
UPDATES = 2
PRIOR_STEPS = 100
MB = 288
ROWS = 864
KPAD = 896
D = 5120
VW = 512
PIECE = 160
LANES = 128
ROW_TILE = 288

BETA_ONE = 0.9
BETA_TWO = 0.999
LEARN_RATE = 0.001
DECAY_RATE = 0.01
ADAM_EPS = 1e-08
CLIP_EPS = 0.2

PARTS = ((0, 64), (64, 48), (112, 48))
SUM_TYPES = (jnp.float32, jnp.bfloat16)
N_SUMS = 17
CHUNKS_IN = (0, 1, 3, 2)
CHUNKS_OUT = (2, 1, 3, 0)


def adam_step(master, moment_one, moment_two, gradient, step_num):
    moment_one = BETA_ONE * moment_one + (1.0 - BETA_ONE) * gradient
    moment_two = BETA_TWO * moment_two + (1.0 - BETA_TWO) * gradient * gradient
    first_hat = moment_one / (1.0 - BETA_ONE**step_num)
    second_hat = moment_two / (1.0 - BETA_TWO**step_num)
    master = master - LEARN_RATE * (
        first_hat / (jnp.sqrt(second_hat) + ADAM_EPS) + DECAY_RATE * master
    )
    return (master, moment_one, moment_two)


class Sems:
    def __init__(self, send, recv):
        self.send, self.recv, self.index = send, recv, {}

    def pair(self, *name):
        slot = self.index.setdefault(name, len(self.index))
        return self.send.at[slot], self.recv.at[slot]


N_SEMS = 160


def f32(value):
    return value.astype(jnp.float32)


def kernel(
    states_hbm, read_hbm, meta_ref, w_ref, m_ref, v_ref,
    wo_ref, mo_ref, vo_ref,
    st, st_t, rd, wh, acc, sc, gfull, cnt, cnt_in, load_sem, send_sem, recv_sem, *sums,
):
    dp, sh = lax.axis_index("dp"), lax.axis_index("shard")
    xl, z = dp // 4, dp % 4
    y, xh, c = sh // 4, (sh // 2) % 2, sh % 2
    x = xh * 2 + xl

    def device(x_, y_, z_, c_):
        return ((x_ % 2) * 4 + z_, y_ * 4 + (x_ // 2) * 2 + c_)

    def turn(axis, d):
        return ({"x": x, "y": y, "z": z}[axis] + d) % 4

    def peer(axis, d):
        to = turn(axis, d)
        return device(
            to if axis == "x" else x, to if axis == "y" else y, to if axis == "z" else z, c
        )

    twin = device(x, y, z, 1 - c)
    partner = device(xh * 2 + (1 - xl), y, z, c)

    def lanes(index):
        return pl.ds(pl.multiple_of(index * LANES, LANES), LANES)

    zc = lanes(z)
    rows_of = [pl.ds(first, size) for first, size in PARTS]
    sems = Sems(send_sem, recv_sem)

    def send(src, dst, to, *name):
        send_at, recv_at = sems.pair(*name)
        copy = pltpu.make_async_remote_copy(
            src_ref=src, dst_ref=dst, send_sem=send_at, recv_sem=recv_at,
            device_id=to, device_id_type=MESH,
        )
        copy.start()
        return copy

    loads = []
    for k in range(4):
        cols = pl.ds(k * 1280, 1280)
        loads.append(pltpu.make_async_copy(states_hbm.at[:, cols], st.at[:, cols], load_sem.at[k]))
    loads.append(pltpu.make_async_copy(read_hbm, rd, load_sem.at[4]))
    for load in loads:
        load.start()

    barrier = pltpu.get_barrier_semaphore()
    greeted = [peer(axis, d) for axis in "xyz" for d in (1, 2, 3)] + [twin]
    for to in greeted:
        pl.semaphore_signal(barrier, inc=1, device_id=to, device_id_type=MESH)

    own_rows = pl.ds(pl.multiple_of(xl * PIECE, PIECE), PIECE)
    wh[c, y, x, :, zc] = w_ref[own_rows, zc].astype(jnp.bfloat16)
    lane = lax.broadcasted_iota(jnp.int32, (8, LANES), 1)
    cnt[...] = jnp.where(
        lane == 0,
        jnp.sum(meta_ref[:, 2:3], axis=0, keepdims=True),
        jnp.where(lane == 1, jnp.sum(meta_ref[:, 3:4], axis=0, keepdims=True), 0.0),
    )
    sc[pl.ds(ROWS, KPAD - ROWS), :] = jnp.zeros((KPAD - ROWS, VW), jnp.bfloat16)
    pl.semaphore_wait(barrier, len(greeted))

    def count_start(stage, axis):
        return [
            send(cnt, cnt_in.at[stage, d - 1], peer(axis, d), "cnt", stage, d) for d in (1, 2, 3)
        ]

    def count_end(stage, copies):
        for copy in copies:
            copy.wait()
        total = cnt[...]
        for d in range(3):
            total = total + cnt_in[stage, d]
        cnt[...] = total

    def transpose_chunk(k):
        loads[k].wait()

        def step(j, carry):
            cols = pl.ds(pl.multiple_of(k * 1280 + j * LANES, LANES), LANES)
            block = jnp.concatenate(
                [st[:, cols], jnp.zeros((KPAD - ROWS, LANES), jnp.bfloat16)], axis=0
            )
            st_t[cols, :] = block.T
            return carry

        lax.fori_loop(0, 10, step, 0)

    def fwd_chunk(yy, first):
        def step(i, carry):
            rows = pl.ds(pl.multiple_of(i * ROW_TILE, ROW_TILE), ROW_TILE)
            weight = jnp.concatenate(
                [
                    wh[core, yy, pl.ds(2 * half, 2)].reshape(2 * PIECE, VW)
                    for half in (0, 1)
                    for core in (0, 1)
                ],
                axis=0,
            )
            cols = pl.ds(pl.multiple_of(yy * 1280, 1280), 1280)
            proj = jnp.dot(st[rows, cols], weight, preferred_element_type=jnp.float32)
            prod = proj * f32(rd[rows, :])
            part = (
                prod[:, 0:128] + prod[:, 128:256] + prod[:, 256:384] + prod[:, 384:512]
            )
            if first:
                acc[rows, :] = part
            else:
                acc[rows, :] += part
            return carry

        lax.fori_loop(0, ROWS // ROW_TILE, step, 0)

    def scale_rows(u):
        total = jnp.maximum(cnt[0:1, u : u + 1], 1.0)

        def step(i, carry):
            rows = pl.ds(pl.multiple_of(i * ROW_TILE, ROW_TILE), ROW_TILE)
            shift, adv = meta_ref[rows, 0:1], meta_ref[rows, 1:2]
            weights = meta_ref[rows, 2 + u : 3 + u]
            log_ratio = shift + jnp.sum(acc[rows, :], axis=1, keepdims=True)
            ratio = jnp.exp(log_ratio)
            clipped = jnp.clip(ratio, 1.0 - CLIP_EPS, 1.0 + CLIP_EPS)
            chosen = ratio * adv <= clipped * adv
            coeff = jnp.where(
                (weights > 0.0) & chosen, -(weights / total) * adv * ratio, 0.0
            )
            sc[rows, :] = (coeff * f32(rd[rows, :])).astype(jnp.bfloat16)
            return carry

        lax.fori_loop(0, ROWS // ROW_TILE, step, 0)

    def grad_half(core, yy, half):
        first = pl.multiple_of(yy * 1280 + half * 640 + core * 320, 320)
        return jnp.dot(
            st_t[pl.ds(first, 320), :], sc[...], preferred_element_type=jnp.float32
        )

    for u in range(UPDATES):
        sent = []
        first_axes, second_axes = "zxy", "xyz"
        hop = {}
        for p in range(3):
            block = wh.at[c, y, x, rows_of[p], zc]
            hop[p] = [
                send(block, block, peer(first_axes[p], d), "ag1", p, d) for d in (1, 2, 3)
            ]
            sent += hop[p]
        if u == 0:
            counting = count_start(0, "z")
            transpose_chunk(0)
        for p in range(3):
            for copy in hop[p]:
                copy.wait_recv()
            block = (
                wh.at[c, y, x, rows_of[p], :],
                wh.at[c, y, :, rows_of[p], zc],
                wh.at[c, :, x, rows_of[p], zc],
            )[p]
            hop[p] = [
                send(block, block, peer(second_axes[p], d), "ag2", p, d) for d in (1, 2, 3)
            ]
            sent += hop[p]
        if u == 0:
            count_end(0, counting)
            counting = count_start(1, "x")
            transpose_chunk(1)
        for p in range(3):
            for copy in hop[p]:
                copy.wait_recv()
        arrive = {o: [] for o in CHUNKS_IN}
        for o in CHUNKS_IN:
            yy = (y + o) % 4
            if o == 0:
                block = wh.at[c, y, :, rows_of[0], :]
                for d in (1, 3, 2):
                    arrive[(4 - d) % 4].append(send(block, block, peer("y", d), "ag3", 0, d))
            block = wh.at[c, yy, :, rows_of[1], zc]
            arrive[o] += [
                send(block, block, peer("z", d), "ag3", 1, o, d) for d in (1, 2, 3)
            ]
            block = wh.at[c, yy, x, rows_of[2], :]
            arrive[o] += [
                send(block, block, peer("x", d), "ag3", 2, o, d) for d in (1, 2, 3)
            ]
        if u == 0:
            count_end(1, counting)
            counting = count_start(2, "y")
            transpose_chunk(2)
            transpose_chunk(3)
            count_end(2, counting)
            counting = [send(cnt, cnt_in.at[3, 0], twin, "cnt", 3)]
            loads[4].wait()
        else:
            block = gfull.at[0, own_rows, zc]
            shared = [send(block, block, peer("z", d), "gz", 0, d) for d in (1, 2, 3)]
            crossed = send(block, block, partner, "gx", 0)

        across = {}
        for i, o in enumerate(CHUNKS_IN):
            ahead = CHUNKS_IN[: 2] if i == 0 else CHUNKS_IN[i + 1 : i + 2]
            for a in ahead:
                for copy in arrive[a]:
                    copy.wait_recv()
                    sent.append(copy)
                block = wh.at[c, (y + a) % 4]
                across[a] = send(block, block, twin, "agc", a)
            across[o].wait_recv()
            fwd_chunk((y + o) % 4, i == 0)
        if u == 0:
            counting[0].wait()
            cnt[...] = cnt[...] + cnt_in[3, 0]
        else:
            crossed.wait()
            block = gfull.at[0, pl.ds(pl.multiple_of((1 - xl) * PIECE, PIECE), PIECE), zc]
            shared += [send(block, block, peer("z", d), "gy", 0, d) for d in (1, 2, 3)]
        scale_rows(u)
        for copy in sent:
            copy.wait_send()
        for o in CHUNKS_IN:
            across[o].wait_send()

        sent = []
        kind = SUM_TYPES[u]
        gsend, gs, r0, r1, r2, s0, s1, s2, q0, q1, q2, t0, t1, t2, e0, e1, e2 = sums[
            N_SUMS * u : N_SUMS * (u + 1)
        ]

        def give(i, given):
            yy = (y + CHUNKS_OUT[i]) % 4
            if i >= 2:
                given[i - 2].wait_send()
            for half in (0, 1):
                gsend[i % 2, pl.ds(2 * half, 2)] = (
                    grad_half(1 - c, yy, half).astype(kind).reshape(2, PIECE, VW)
                )
            given.append(send(gsend.at[i % 2], gs.at[yy], twin, "rsc", i))

        def keep(i, given):
            yy = (y + CHUNKS_OUT[i]) % 4
            given[i].wait_recv()
            for half in (0, 1):
                other = gs[yy, pl.ds(2 * half, 2)].reshape(2 * PIECE, VW)
                gs[yy, pl.ds(2 * half, 2)] = (
                    (grad_half(c, yy, half) + f32(other)).astype(kind).reshape(2, PIECE, VW)
                )

        def first_sends(o):
            yy = (y + o) % 4
            out = {0: [], 1: [], 2: []}
            if o:
                out[0].append(
                    send(gs.at[yy, :, rows_of[0], :], r0.at[o - 1], peer("y", o), "rs1", 0, o)
                )
            for d in (1, 2, 3):
                out[1].append(
                    send(
                        gs.at[yy, :, rows_of[1], lanes(turn("z", d))], r1.at[d - 1, yy],
                        peer("z", d), "rs1", 1, o, d,
                    )
                )
                out[2].append(
                    send(
                        gs.at[yy, turn("x", d), rows_of[2], :], r2.at[d - 1, yy],
                        peer("x", d), "rs1", 2, o, d,
                    )
                )
            return out

        def add_up(own, parts):
            total = f32(own)
            for part in parts:
                total = total + f32(part)
            return total

        def first_sums(o, out):
            yy = (y + o) % 4
            for copy in out[1] + out[2]:
                copy.wait_recv()
            s1[yy] = add_up(gs[yy, :, rows_of[1], zc], [r1[d, yy] for d in range(3)]).astype(kind)
            s2[yy] = add_up(gs[yy, x, rows_of[2], :], [r2[d, yy] for d in range(3)]).astype(kind)

        given = []
        give(0, given)
        outs = {}
        for i, o in enumerate(CHUNKS_OUT):
            if i + 1 < 4:
                give(i + 1, given)
            keep(i, given)
            outs[o] = first_sends(o)
            if i:
                first_sums(CHUNKS_OUT[i - 1], outs[CHUNKS_OUT[i - 1]])
        for o in (1, 2, 3):
            outs[o][0][0].wait_recv()
        for xx in range(4):
            s0[xx] = add_up(gs[y, xx, rows_of[0], :], [r0[d, xx] for d in range(3)]).astype(kind)
        hop = {0: [], 1: [], 2: []}
        for d in (1, 2, 3):
            hop[0].append(send(s0.at[turn("x", d)], q0.at[d - 1], peer("x", d), "rs2", 0, d))
        first_sums(CHUNKS_OUT[3], outs[CHUNKS_OUT[3]])
        for d in (1, 2, 3):
            hop[1].append(send(s1.at[turn("y", d)], q1.at[d - 1], peer("y", d), "rs2", 1, d))
            hop[2].append(
                send(s2.at[:, :, lanes(turn("z", d))], q2.at[d - 1], peer("z", d), "rs2", 2, d)
            )
        for o in CHUNKS_OUT:
            sent += outs[o][0] + outs[o][1] + outs[o][2]
        sent += given[2:]
        for p in range(3):
            for copy in hop[p]:
                copy.wait_recv()
            sent += hop[p]
            hop[p] = []
            if p == 0:
                t0[...] = add_up(s0[x], [q0[d] for d in range(3)]).astype(kind)
                for d in (1, 2, 3):
                    hop[0].append(
                        send(t0.at[:, lanes(turn("z", d))], e0.at[d - 1], peer("z", d), "rs3", 0, d)
                    )
            elif p == 1:
                t1[...] = add_up(s1[y], [q1[d] for d in range(3)]).astype(kind)
                for d in (1, 2, 3):
                    hop[1].append(
                        send(t1.at[turn("x", d)], e1.at[d - 1], peer("x", d), "rs3", 1, d)
                    )
            else:
                t2[...] = add_up(s2[:, :, zc], [q2[d] for d in range(3)]).astype(kind)
                for d in (1, 2, 3):
                    hop[2].append(
                        send(t2.at[turn("y", d)], e2.at[d - 1], peer("y", d), "rs3", 2, d)
                    )
        for p in range(3):
            for copy in hop[p]:
                copy.wait_recv()
            sent += hop[p]
        gradient = jnp.concatenate(
            [
                add_up(t0[:, zc], [e0[d] for d in range(3)]),
                add_up(t1[x], [e1[d] for d in range(3)]),
                add_up(t2[y], [e2[d] for d in range(3)]),
            ],
            axis=0,
        )
        gfull[u, own_rows, zc] = gradient
        if u == 0:
            master, _, _ = adam_step(
                w_ref[own_rows, zc], m_ref[own_rows, zc], v_ref[own_rows, zc],
                gradient, PRIOR_STEPS + 1,
            )
            wh[c, y, x, :, zc] = master.astype(jnp.bfloat16)
        else:
            block = gfull.at[1, own_rows, zc]
            last = [send(block, block, partner, "gx", 1)]
            shared += [send(block, block, peer("z", d), "gz", 1, d) for d in (1, 2, 3)]
            last[0].wait_recv()
            block = gfull.at[1, pl.ds(pl.multiple_of((1 - xl) * PIECE, PIECE), PIECE), zc]
            shared += [send(block, block, peer("z", d), "gy", 1, d) for d in (1, 2, 3)]
            for copy in shared:
                copy.wait_recv()
            sent += shared + last
        for copy in sent:
            copy.wait_send()

    def finish(i, carry):
        rows = pl.ds(pl.multiple_of(i * 32, 32), 32)
        master, one, two = w_ref[rows, :], m_ref[rows, :], v_ref[rows, :]
        for u in range(UPDATES):
            master, one, two = adam_step(master, one, two, gfull[u, rows, :], PRIOR_STEPS + u + 1)
        wo_ref[rows, :] = master
        mo_ref[rows, :] = one
        vo_ref[rows, :] = two
        return carry

    lax.fori_loop(0, 10, finish, 0)


def body(
    states, readout, logp_shift, advantage, response_mask, rollout_len, dest_slot,
    weight, moment1, moment2,
):
    row_index = jnp.arange(ROWS, dtype=jnp.int32)
    live = (row_index < rollout_len[0]) & (dest_slot >= 0)
    batch = jnp.where(live, (dest_slot % BAL) // MB, UPDATES)
    token = response_mask.astype(jnp.float32)
    meta = jnp.stack(
        [logp_shift.astype(jnp.float32), advantage.astype(jnp.float32)]
        + [jnp.where(batch == k, token, 0.0) for k in range(UPDATES)],
        axis=1,
    )
    bf16, full = jnp.bfloat16, jnp.float32
    vmem = pl.BlockSpec(memory_space=pltpu.VMEM)
    hbm = pl.BlockSpec(memory_space=pl.ANY)
    a, b, d = [size for _, size in PARTS]
    sums = [
        (2, 4, PIECE, VW), (4, 4, PIECE, VW),
        (3, 4, a, VW), (3, 4, 4, b, LANES), (3, 4, d, VW),
        (4, a, VW), (4, 4, b, LANES), (4, d, VW),
        (3, a, VW), (3, 4, b, LANES), (3, 4, d, LANES),
        (a, VW), (4, b, LANES), (4, d, LANES),
        (3, a, LANES), (3, b, LANES), (3, d, LANES),
    ]
    shard = jax.ShapeDtypeStruct(weight.shape, full)
    return pl.pallas_call(
        kernel,
        out_shape=(shard, shard, shard),
        in_specs=[hbm, hbm, vmem, vmem, vmem, vmem],
        out_specs=(vmem, vmem, vmem),
        scratch_shapes=[
            pltpu.VMEM((ROWS, D), bf16),
            pltpu.VMEM((D, KPAD), bf16),
            pltpu.VMEM((ROWS, VW), bf16),
            pltpu.VMEM((2, 4, 4, PIECE, VW), bf16),
            pltpu.VMEM((ROWS, LANES), full),
            pltpu.VMEM((KPAD, VW), bf16),
            pltpu.VMEM((2, 2 * PIECE, VW), full),
            pltpu.VMEM((8, LANES), full),
            pltpu.VMEM((4, 3, 8, LANES), full),
            pltpu.SemaphoreType.DMA((5,)),
            pltpu.SemaphoreType.DMA((N_SEMS,)),
            pltpu.SemaphoreType.DMA((N_SEMS,)),
        ]
        + [pltpu.VMEM(dims, kind) for kind in SUM_TYPES for dims in sums],
        compiler_params=pltpu.CompilerParams(
            collective_id=0, has_side_effects=True, vmem_limit_bytes=58 * 1024 * 1024
        ),
    )(states, readout, meta, weight, moment1, moment2)


def solution(mesh):
    rows = P(("dp", "shard"))
    return jax.shard_map(
        body,
        mesh=mesh,
        in_specs=(
            P(("dp", "shard"), None), P(("dp", "shard"), None), rows, rows, rows, rows, rows,
            P("shard", None), P("shard", None), P("shard", None),
        ),
        out_specs=(P("shard", None), P("shard", None), P("shard", None)),
        check_vma=False,
    )
```

```python
import jax
import jax.numpy as jnp
from jax import lax
from jax.experimental import pallas as pl
from jax.experimental.pallas import tpu as pltpu
from jax.sharding import PartitionSpec as P

MESH = pl.DeviceIdType.MESH

BAL = 576
UPDATES = 2
PRIOR_STEPS = 100
MB = 288
ROWS = 864
KPAD = 896
D = 5120
VW = 512
PIECE = 160
LANES = 128
ROW_TILE = 288

BETA_ONE = 0.9
BETA_TWO = 0.999
LEARN_RATE = 0.001
DECAY_RATE = 0.01
ADAM_EPS = 1e-08
CLIP_EPS = 0.2

PARTS = ((0, 64), (64, 48), (112, 48))
SUM_TYPES = (jnp.float32, jnp.bfloat16)
N_SUMS = 18
CHUNKS_IN = (0, 1, 3, 2)
CHUNKS_OUT = (2, 1, 3, 0)


def adam_step(master, moment_one, moment_two, gradient, step_num):
    moment_one = BETA_ONE * moment_one + (1.0 - BETA_ONE) * gradient
    moment_two = BETA_TWO * moment_two + (1.0 - BETA_TWO) * gradient * gradient
    first_hat = moment_one / (1.0 - BETA_ONE**step_num)
    second_hat = moment_two / (1.0 - BETA_TWO**step_num)
    master = master - LEARN_RATE * (
        first_hat / (jnp.sqrt(second_hat) + ADAM_EPS) + DECAY_RATE * master
    )
    return (master, moment_one, moment_two)


class Sems:
    def __init__(self, send, recv):
        self.send, self.recv, self.index = send, recv, {}

    def pair(self, *name):
        slot = self.index.setdefault(name, len(self.index))
        return self.send.at[slot], self.recv.at[slot]


N_SEMS = 200


def f32(value):
    return value.astype(jnp.float32)


def kernel(
    states_hbm, read_hbm, meta_ref, w_hbm, m_hbm, v_hbm, out_ref,
    st, st_t, rd, meta, w_ref, m_ref, v_ref, wh, acc, sc, cnt, cnt_in,
    load_sem, send_sem, recv_sem, *sums,
):
    dp, sh = lax.axis_index("dp"), lax.axis_index("shard")
    xl, z = dp // 4, dp % 4
    y, xh, c = sh // 4, (sh // 2) % 2, sh % 2
    x = xh * 2 + xl

    def device(x_, y_, z_, c_):
        return ((x_ % 2) * 4 + z_, y_ * 4 + (x_ // 2) * 2 + c_)

    def turn(axis, d):
        return ({"x": x, "y": y, "z": z}[axis] + d) % 4

    def peer(axis, d):
        to = turn(axis, d)
        return device(
            to if axis == "x" else x, to if axis == "y" else y, to if axis == "z" else z, c
        )

    twin = device(x, y, z, 1 - c)
    pair = xh * 2 + (1 - xl)
    replicas = [device(pair, y, turn("z", d), c) for d in range(4)]
    across_xy = [device(turn("x", 2), turn("y", d), z, c) for d in range(4)]

    def lanes(index):
        return pl.ds(pl.multiple_of(index * LANES, LANES), LANES)

    zc = lanes(z)
    rows_of = [pl.ds(first, size) for first, size in PARTS]
    sems = Sems(send_sem, recv_sem)

    def send(src, dst, to, *name):
        send_at, recv_at = sems.pair(*name)
        copy = pltpu.make_async_remote_copy(
            src_ref=src, dst_ref=dst, send_sem=send_at, recv_sem=recv_at,
            device_id=to, device_id_type=MESH,
        )
        copy.start()
        return copy

    own_rows = pl.ds(pl.multiple_of(xl * PIECE, PIECE), PIECE)

    loads = [pltpu.make_async_copy(w_hbm, w_ref, load_sem.at[0])]
    for k in range(4):
        cols = pl.ds(k * 1280, 1280)
        loads.append(
            pltpu.make_async_copy(states_hbm.at[:, cols], st.at[:, cols], load_sem.at[1 + k])
        )
    loads.append(pltpu.make_async_copy(read_hbm, rd, load_sem.at[5]))
    loads.append(pltpu.make_async_copy(m_hbm.at[own_rows, zc], m_ref, load_sem.at[6]))
    loads.append(pltpu.make_async_copy(v_hbm.at[own_rows, zc], v_ref, load_sem.at[7]))
    for load in loads:
        load.start()

    barrier = pltpu.get_barrier_semaphore()
    greeted = [peer(axis, d) for axis in "xyz" for d in (1, 2, 3)] + [twin]
    greeted += replicas[1:] + across_xy[1:]
    for to in greeted:
        pl.semaphore_signal(barrier, inc=1, device_id=to, device_id_type=MESH)

    meta[...] = meta_ref[...].T
    lane = lax.broadcasted_iota(jnp.int32, (8, LANES), 1)
    cnt[...] = jnp.where(
        lane == 0,
        jnp.sum(meta_ref[2:3, :], axis=1, keepdims=True),
        jnp.where(lane == 1, jnp.sum(meta_ref[3:4, :], axis=1, keepdims=True), 0.0),
    )
    sc[pl.ds(ROWS, KPAD - ROWS), :] = jnp.zeros((KPAD - ROWS, VW), jnp.bfloat16)
    loads[0].wait()
    for p in (0, 2):
        first, size = PARTS[p]
        rows = pl.ds(pl.multiple_of(xl * PIECE + first, 16), size)
        wh[c, y, x, rows_of[p], :] = w_ref[rows, :].astype(jnp.bfloat16)
    for half in range(2):
        first, size = PARTS[1]
        rows = pl.ds(half * PIECE + first, size)
        wh[c, y, 2 * xh + half, rows_of[1], zc] = w_ref[rows, zc].astype(jnp.bfloat16)
    pl.semaphore_wait(barrier, len(greeted))

    def count_start(stage, axis):
        return [
            send(cnt, cnt_in.at[stage, d - 1], peer(axis, d), "cnt", stage, d) for d in (1, 2, 3)
        ]

    def count_end(stage, copies):
        for copy in copies:
            copy.wait()
        total = cnt[...]
        for d in range(3):
            total = total + cnt_in[stage, d]
        cnt[...] = total

    def transpose_chunk(k):
        loads[1 + k].wait()

        def step(j, carry):
            cols = pl.ds(pl.multiple_of(k * 1280 + j * LANES, LANES), LANES)
            block = jnp.concatenate(
                [st[:, cols], jnp.zeros((KPAD - ROWS, LANES), jnp.bfloat16)], axis=0
            )
            st_t[cols, :] = block.T
            return carry

        lax.fori_loop(0, 10, step, 0)

    def fwd_chunk(yy, first):
        def step(i, carry):
            rows = pl.ds(pl.multiple_of(i * ROW_TILE, ROW_TILE), ROW_TILE)
            weight = jnp.concatenate(
                [
                    wh[core, yy, pl.ds(2 * half, 2)].reshape(2 * PIECE, VW)
                    for half in (0, 1)
                    for core in (0, 1)
                ],
                axis=0,
            )
            cols = pl.ds(pl.multiple_of(yy * 1280, 1280), 1280)
            proj = jnp.dot(st[rows, cols], weight, preferred_element_type=jnp.float32)
            prod = proj * f32(rd[rows, :])
            part = (
                prod[:, 0:128] + prod[:, 128:256] + prod[:, 256:384] + prod[:, 384:512]
            )
            if first:
                acc[rows, :] = part
            else:
                acc[rows, :] += part
            return carry

        lax.fori_loop(0, ROWS // ROW_TILE, step, 0)

    def scale_rows(u):
        total = jnp.maximum(cnt[0:1, u : u + 1], 1.0)

        def step(i, carry):
            rows = pl.ds(pl.multiple_of(i * ROW_TILE, ROW_TILE), ROW_TILE)
            shift, adv = meta[rows, 0:1], meta[rows, 1:2]
            weights = meta[rows, 2 + u : 3 + u]
            log_ratio = shift + jnp.sum(acc[rows, :], axis=1, keepdims=True)
            ratio = jnp.exp(log_ratio)
            clipped = jnp.clip(ratio, 1.0 - CLIP_EPS, 1.0 + CLIP_EPS)
            chosen = ratio * adv <= clipped * adv
            coeff = jnp.where(
                (weights > 0.0) & chosen, -(weights / total) * adv * ratio, 0.0
            )
            sc[rows, :] = (coeff * f32(rd[rows, :])).astype(jnp.bfloat16)
            return carry

        lax.fori_loop(0, ROWS // ROW_TILE, step, 0)

    def grad_half(core, yy, half):
        first = pl.multiple_of(yy * 1280 + half * 640 + core * 320, 320)
        return jnp.dot(
            st_t[pl.ds(first, 320), :], sc[...], preferred_element_type=jnp.float32
        )

    def add_up(own, parts):
        total = f32(own)
        for part in parts:
            total = total + f32(part)
        return total

    def share(u):
        block = out_ref.at[u, own_rows, zc]
        return [send(block, block, peer("z", d), "share", u, 0, d) for d in (1, 2, 3)] + [
            send(block, block, replicas[d], "share", u, 1, d) for d in range(4)
        ]

    shared = []
    for u in range(UPDATES):
        sent = []

        def ring(axis, block, *name):
            copies = [send(block, block, peer(axis, d), *name, d) for d in (1, 3, 2)]
            sent.extend(copies)
            return dict(zip((1, 3, 2), copies))

        def along_y(j):
            block = wh.at[c, y, turn("x", -j), rows_of[0], :]
            return {d: send(block, block, peer("y", d), "ag3", 0, j, d) for d in (1, 3)}

        whole = wh.at[c, y, x, rows_of[0], :]
        part_y, part_z, part_x = {}, {}, {}
        if u == 0:
            second = {0: ring("x", whole, "ag2", 0)}
            both = wh.at[c, y, pl.ds(2 * xh, 2), rows_of[1], zc]
            plane = [send(both, both, across_xy[0], "ag2", 1, 0)]
            plane += [send(both, both, peer("y", d), "ag2", 1, 1, d) for d in (1, 2, 3)]
            plane += [send(both, both, across_xy[d], "ag2", 1, 2, d) for d in (1, 2, 3)]
            sent += plane
            second[2] = ring("y", wh.at[c, y, x, rows_of[2], :], "ag2", 2)
            part_y[0] = along_y(0)
            counting = count_start(0, "z")
            transpose_chunk(0)
            count_end(0, counting)
            counting = count_start(1, "x")
            for copy in plane:
                copy.wait_recv()
            part_z[0] = ring("z", wh.at[c, y, :, rows_of[1], zc], "ag3", 1, 0)
        else:
            first = [
                ring(axis, wh.at[c, y, x, rows_of[p], zc], "ag1", p)
                for p, axis in enumerate("zxy")
            ]
            second = {}
            for copy in first[0].values():
                copy.wait_recv()
            second[0] = ring("x", whole, "ag2", 0)
            for copy in first[1].values():
                copy.wait_recv()
            second[1] = ring("y", wh.at[c, y, :, rows_of[1], zc], "ag2", 1)
            for copy in first[2].values():
                copy.wait_recv()
            second[2] = ring("z", wh.at[c, :, x, rows_of[2], zc], "ag2", 2)
            part_y[0] = along_y(0)
            part_z[0] = ring("z", wh.at[c, y, :, rows_of[1], zc], "ag3", 1, 0)
        for d in (1, 3):
            second[0][d].wait_recv()
            part_y[d] = along_y(d)
        if u == 1:
            for copy in second[2].values():
                copy.wait_recv()
        part_x[0] = ring("x", wh.at[c, y, x, rows_of[2], :], "ag3", 2, 0)
        second[0][2].wait_recv()
        part_y[2] = along_y(2)
        for o in (1, 3, 2):
            yy = (y + o) % 4
            if u == 1:
                second[1][4 - o].wait_recv()
            part_z[o] = ring("z", wh.at[c, yy, :, rows_of[1], zc], "ag3", 1, o)
            if u == 0:
                second[2][4 - o].wait_recv()
            part_x[o] = ring("x", wh.at[c, yy, x, rows_of[2], :], "ag3", 2, o)
        if u == 0:
            transpose_chunk(1)
            count_end(1, counting)
            counting = count_start(2, "y")

        relays = []
        for j, d in ((0, 1), (1, 1), (3, 3), (2, 3)):
            part_y[j][d].wait_recv()
            block = wh.at[c, turn("y", -d), turn("x", -j), rows_of[0], :]
            relays.append(send(block, block, peer("y", d), "ag4", j))

        def arrived(o):
            if o == 2:
                for copy in relays:
                    copy.wait_recv()
            elif o:
                for j in range(4):
                    if (j, 4 - o) not in ((0, 1), (1, 1), (3, 3), (2, 3)):
                        part_y[j][4 - o].wait_recv()
            for copy in list(part_z[o].values()) + list(part_x[o].values()):
                copy.wait_recv()

        if u == 0:
            transpose_chunk(2)
            transpose_chunk(3)
            count_end(2, counting)
            counting = [send(cnt, cnt_in.at[3, 0], twin, "cnt", 3)]
            loads[5].wait()
        across = {}
        for i, o in enumerate(CHUNKS_IN):
            for a in CHUNKS_IN[:2] if i == 0 else CHUNKS_IN[i + 1 : i + 2]:
                arrived(a)
                block = wh.at[c, (y + a) % 4]
                across[a] = send(block, block, twin, "agc", a)
                if u == 1 and a == CHUNKS_IN[3]:
                    shared += share(0)
            across[o].wait_recv()
            fwd_chunk((y + o) % 4, i == 0)
        if u == 0:
            counting[0].wait()
            cnt[...] = cnt[...] + cnt_in[3, 0]
        scale_rows(u)
        for j in range(4):
            sent += part_y[j].values()
        sent += relays
        sent += across.values()
        for copy in sent:
            copy.wait_send()

        sent = []
        kind = SUM_TYPES[u]
        gsend, gs, rel, r0, r1, r2, s0, s1, s2, q0, q1, q2, t0, t1, t2, e0, e1, e2 = sums[
            N_SUMS * u : N_SUMS * (u + 1)
        ]

        def give(i, given):
            yy = (y + CHUNKS_OUT[i]) % 4
            if i >= 2:
                given[i - 2].wait_send()
            for half in (0, 1):
                gsend[i % 2, pl.ds(2 * half, 2)] = (
                    grad_half(1 - c, yy, half).astype(kind).reshape(2, PIECE, VW)
                )
            given.append(send(gsend.at[i % 2], gs.at[yy], twin, "rsc", i))

        def keep(i, given):
            yy = (y + CHUNKS_OUT[i]) % 4
            given[i].wait_recv()
            for half in (0, 1):
                other = gs[yy, pl.ds(2 * half, 2)].reshape(2 * PIECE, VW)
                gs[yy, pl.ds(2 * half, 2)] = (
                    (grad_half(c, yy, half) + f32(other)).astype(kind).reshape(2, PIECE, VW)
                )

        def first_sends(o):
            yy = (y + o) % 4
            for d in (2, 1, 3):
                outs[1, o, d] = send(
                    gs.at[yy, :, rows_of[1], lanes(turn("z", d))], r1.at[d - 1, yy],
                    peer("z", d), "rs1", 1, o, d,
                )
                outs[2, o, d] = send(
                    gs.at[yy, turn("x", d), rows_of[2], :], r2.at[d - 1, yy],
                    peer("x", d), "rs1", 2, o, d,
                )

        def first_sums(o):
            yy = (y + o) % 4
            for d in (1, 2, 3):
                outs[1, o, d].wait_recv()
            s1[yy] = add_up(gs[yy, :, rows_of[1], zc], [r1[d, yy] for d in range(3)]).astype(kind)
            if o:
                hop[1].append(send(s1.at[yy], q1.at[o - 1], peer("y", o), "rs2", 1, o))
            for d in (1, 2, 3):
                outs[2, o, d].wait_recv()
            s2[yy] = add_up(gs[yy, x, rows_of[2], :], [r2[d, yy] for d in range(3)]).astype(kind)
            for d in (2, 1, 3):
                hop[2].append(
                    send(
                        s2.at[yy, :, lanes(turn("z", d))], q2.at[d - 1, yy], peer("z", d),
                        "rs2", 2, o, d,
                    )
                )

        def pass_on(o):
            yy = (y + o) % 4
            side = 0 if o == 1 else 1
            relayed[side].wait_recv()
            for k in range(2):
                gs[yy, 2 * side + k, rows_of[0], :] = (
                    f32(gs[yy, 2 * side + k, rows_of[0], :]) + f32(rel[side, k])
                ).astype(kind)
            outs[0, o, 0] = send(
                gs.at[yy, :, rows_of[0], :], r0.at[side], peer("y", o), "rs1", 0, o
            )

        given, outs, hop = [], {}, {0: [], 1: [], 2: []}
        give(0, given)
        for i, o in enumerate(CHUNKS_OUT):
            if i + 1 < 4:
                give(i + 1, given)
            keep(i, given)
            if i == 0:
                relayed = [
                    send(
                        gs.at[turn("y", 2), pl.ds(2 * side, 2), rows_of[0], :], rel.at[side],
                        peer("y", 1 + 2 * side), "rs0", side,
                    )
                    for side in range(2)
                ]
            first_sends(o)
            if i >= 2:
                pass_on(CHUNKS_OUT[i - 1])
            if i:
                first_sums(CHUNKS_OUT[i - 1])
        first_sums(CHUNKS_OUT[3])
        for o in (1, 3):
            outs[0, o, 0].wait_recv()
        for d in (2, 1, 3, 0):
            xx = turn("x", d)
            s0[xx] = add_up(gs[y, xx, rows_of[0], :], [r0[0, xx], r0[1, xx]]).astype(kind)
            if d:
                hop[0].append(send(s0.at[xx], q0.at[d - 1], peer("x", d), "rs2", 0, d))
        sent += relayed + given[2:]
        sent += outs.values()
        last = {}
        for p in (1, 2, 0):
            for copy in hop[p]:
                copy.wait_recv()
            sent += hop[p]
            if p == 0:
                t0[...] = add_up(s0[x], [q0[d] for d in range(3)]).astype(kind)
                last[0] = [
                    send(t0.at[:, lanes(turn("z", d))], e0.at[d - 1], peer("z", d), "rs3", 0, d)
                    for d in (2, 1, 3)
                ]
            elif p == 1:
                t1[...] = add_up(s1[y], [q1[d] for d in range(3)]).astype(kind)
                last[1] = [
                    send(t1.at[turn("x", d)], e1.at[d - 1], peer("x", d), "rs3", 1, d)
                    for d in (2, 1, 3)
                ]
            else:
                t2[...] = add_up(s2[:, :, zc], [q2[d] for d in range(3)]).astype(kind)
                last[2] = [
                    send(t2.at[turn("y", d)], e2.at[d - 1], peer("y", d), "rs3", 2, d)
                    for d in (2, 1, 3)
                ]
        for p in (1, 2, 0):
            for copy in last[p]:
                copy.wait_recv()
            sent += last[p]
        gradient = jnp.concatenate(
            [
                add_up(t0[:, zc], [e0[d] for d in range(3)]),
                add_up(t1[x], [e1[d] for d in range(3)]),
                add_up(t2[y], [e2[d] for d in range(3)]),
            ],
            axis=0,
        )
        out_ref[u, own_rows, zc] = gradient.astype(jnp.bfloat16)
        if u == 0:
            for load in loads[6:]:
                load.wait()
            master, _, _ = adam_step(
                w_ref[own_rows, zc], m_ref[...], v_ref[...], gradient, PRIOR_STEPS + 1
            )
            wh[c, y, x, :, zc] = master.astype(jnp.bfloat16)
        else:
            shared += share(1)
            for copy in shared:
                copy.wait_recv()
            sent += shared
        for copy in sent:
            copy.wait_send()


def body(
    states, readout, logp_shift, advantage, response_mask, rollout_len, dest_slot,
    weight, moment1, moment2,
):
    row_index = jnp.arange(ROWS, dtype=jnp.int32)
    live = (row_index < rollout_len[0]) & (dest_slot >= 0)
    batch = jnp.where(live, (dest_slot % BAL) // MB, UPDATES)
    token = response_mask.astype(jnp.float32)
    lines = [logp_shift.astype(jnp.float32), advantage.astype(jnp.float32)]
    lines += [jnp.where(batch == k, token, 0.0) for k in range(UPDATES)]
    meta = jnp.pad(jnp.stack(lines), ((0, 4), (0, KPAD - ROWS)))
    bf16, full = jnp.bfloat16, jnp.float32
    vmem = pl.BlockSpec(memory_space=pltpu.VMEM)
    hbm = pl.BlockSpec(memory_space=pl.ANY)
    a, b, d = [size for _, size in PARTS]
    sums = [
        (2, 4, PIECE, VW), (4, 4, PIECE, VW), (2, 2, a, VW),
        (2, 4, a, VW), (3, 4, 4, b, LANES), (3, 4, d, VW),
        (4, a, VW), (4, 4, b, LANES), (4, d, VW),
        (3, a, VW), (3, 4, b, LANES), (3, 4, d, LANES),
        (a, VW), (4, b, LANES), (4, d, LANES),
        (3, a, LANES), (3, b, LANES), (3, d, LANES),
    ]
    gradients = pl.pallas_call(
        kernel,
        out_shape=jax.ShapeDtypeStruct((UPDATES,) + weight.shape, bf16),
        in_specs=[hbm, hbm, vmem, hbm, hbm, hbm],
        out_specs=vmem,
        scratch_shapes=[
            pltpu.VMEM((ROWS, D), bf16),
            pltpu.VMEM((D, KPAD), bf16),
            pltpu.VMEM((ROWS, VW), bf16),
            pltpu.VMEM((KPAD, 8), full),
            pltpu.VMEM((2 * PIECE, VW), full),
            pltpu.VMEM((PIECE, LANES), full),
            pltpu.VMEM((PIECE, LANES), full),
            pltpu.VMEM((2, 4, 4, PIECE, VW), bf16),
            pltpu.VMEM((ROWS, LANES), full),
            pltpu.VMEM((KPAD, VW), bf16),
            pltpu.VMEM((8, LANES), full),
            pltpu.VMEM((4, 3, 8, LANES), full),
            pltpu.SemaphoreType.DMA((8,)),
            pltpu.SemaphoreType.DMA((N_SEMS,)),
            pltpu.SemaphoreType.DMA((N_SEMS,)),
        ]
        + [pltpu.VMEM(dims, kind) for kind in SUM_TYPES for dims in sums],
        compiler_params=pltpu.CompilerParams(
            collective_id=0, has_side_effects=True, vmem_limit_bytes=58 * 1024 * 1024
        ),
    )(states, readout, meta, weight, moment1, moment2)
    master, one, two = weight, moment1, moment2
    for u in range(UPDATES):
        master, one, two = adam_step(
            master, one, two, gradients[u].astype(full), PRIOR_STEPS + u + 1
        )
    return master, one, two


def solution(mesh):
    rows = P(("dp", "shard"))
    return jax.shard_map(
        body,
        mesh=mesh,
        in_specs=(
            P(("dp", "shard"), None), P(("dp", "shard"), None), rows, rows, rows, rows, rows,
            P("shard", None), P("shard", None), P("shard", None),
        ),
        out_specs=(P("shard", None), P("shard", None), P("shard", None)),
        check_vma=False,
    )
```

```python
import jax
import jax.numpy as jnp
from jax import lax
from jax.experimental import pallas as pl
from jax.experimental.pallas import tpu as pltpu
from jax.sharding import PartitionSpec as P

MESH = pl.DeviceIdType.MESH

BAL = 576
UPDATES = 2
PRIOR_STEPS = 100
MB = 288
ROWS = 864
KPAD = 896
D = 5120
VW = 512
PIECE = 160
LANES = 128
ROW_TILE = 288

BETA_ONE = 0.9
BETA_TWO = 0.999
LEARN_RATE = 0.001
DECAY_RATE = 0.01
ADAM_EPS = 1e-08
CLIP_EPS = 0.2

WHOLE = ((0, 64), (64, 48), (112, 48))
STREAMS = (
    (((0, 32), (32, 16), (48, 32)), ((80, 32), (112, 32), (144, 16))),
    (WHOLE,),
)
SUM_TYPES = (jnp.float32, jnp.bfloat16)
CHUNKS_IN = (0, 1, 3, 2)
CHUNKS_OUT = (2, 1, 3, 0)


def adam_step(master, moment_one, moment_two, gradient, step_num):
    moment_one = BETA_ONE * moment_one + (1.0 - BETA_ONE) * gradient
    moment_two = BETA_TWO * moment_two + (1.0 - BETA_TWO) * gradient * gradient
    first_hat = moment_one / (1.0 - BETA_ONE**step_num)
    second_hat = moment_two / (1.0 - BETA_TWO**step_num)
    master = master - LEARN_RATE * (
        first_hat / (jnp.sqrt(second_hat) + ADAM_EPS) + DECAY_RATE * master
    )
    return (master, moment_one, moment_two)


class Sems:
    def __init__(self, send, recv):
        self.send, self.recv, self.index = send, recv, {}

    def pair(self, *name):
        slot = self.index.setdefault(name, len(self.index))
        return self.send.at[slot], self.recv.at[slot]


N_SEMS = 400
N_SUMS = 13


def sums_of(parts):
    (_, a), (_, b), (_, d) = parts
    height = a + b + d
    return [
        (2, 4, height, VW), (4, 4, height, VW), (2, 2, a, VW),
        (2, 4, a, VW), (3, 4, 4, b, LANES), (3, 4, d, VW),
        (4, a, VW), (4, 4, b, LANES), (4, d, VW),
        (4, 4, a, LANES), (4, 4, b, LANES), (4, 4, d, LANES),
        (height, LANES),
    ]


def f32(value):
    return value.astype(jnp.float32)


def kernel(
    states_hbm, read_hbm, meta_ref, w_hbm, m_hbm, v_hbm, out_ref,
    st, st_t, rd, meta, w_ref, m_ref, v_ref, wh, acc, sc, cnt, cnt_in,
    load_sem, send_sem, recv_sem, *sums,
):
    dp, sh = lax.axis_index("dp"), lax.axis_index("shard")
    xl, z = dp // 4, dp % 4
    y, xh, c = sh // 4, (sh // 2) % 2, sh % 2
    x = xh * 2 + xl

    def device(x_, y_, z_, c_):
        return ((x_ % 2) * 4 + z_, y_ * 4 + (x_ // 2) * 2 + c_)

    def turn(axis, d):
        return ({"x": x, "y": y, "z": z}[axis] + d) % 4

    def peer(axis, d):
        to = turn(axis, d)
        return device(
            to if axis == "x" else x, to if axis == "y" else y, to if axis == "z" else z, c
        )

    twin = device(x, y, z, 1 - c)
    pair = xh * 2 + (1 - xl)
    replicas = [device(pair, y, turn("z", d), c) for d in range(4)]
    across_xy = [device(turn("x", 2), turn("y", d), z, c) for d in range(4)]
    flip = (x, pair, turn("x", 2), 3 - x)
    flipped = [device(to, y, z, c) for to in flip]

    def lanes(index):
        return pl.ds(pl.multiple_of(index * LANES, LANES), LANES)

    zc = lanes(z)
    sems = Sems(send_sem, recv_sem)

    def send(src, dst, to, *name):
        send_at, recv_at = sems.pair(*name)
        copy = pltpu.make_async_remote_copy(
            src_ref=src, dst_ref=dst, send_sem=send_at, recv_sem=recv_at,
            device_id=to, device_id_type=MESH,
        )
        copy.start()
        return copy

    own_rows = pl.ds(pl.multiple_of(xl * PIECE, PIECE), PIECE)

    loads = [pltpu.make_async_copy(w_hbm, w_ref, load_sem.at[0])]
    for k in range(4):
        cols = pl.ds(k * 1280, 1280)
        loads.append(
            pltpu.make_async_copy(states_hbm.at[:, cols], st.at[:, cols], load_sem.at[1 + k])
        )
    loads.append(pltpu.make_async_copy(read_hbm, rd, load_sem.at[5]))
    loads.append(pltpu.make_async_copy(m_hbm.at[own_rows, zc], m_ref, load_sem.at[6]))
    loads.append(pltpu.make_async_copy(v_hbm.at[own_rows, zc], v_ref, load_sem.at[7]))
    for load in loads:
        load.start()

    barrier = pltpu.get_barrier_semaphore()
    greeted = [twin]
    for e in range(4):
        for d in range(4):
            if d:
                greeted.append(device(turn("x", d), turn("y", e), z, c))
            if e:
                greeted.append(device(x, turn("y", e), turn("z", d), c))
            if e and d:
                greeted.append(device(turn("x", d), y, turn("z", e), c))
    for d in (1, 2, 3):
        greeted.append(device(x, y, turn("z", d), c))
    for to in greeted:
        pl.semaphore_signal(barrier, inc=1, device_id=to, device_id_type=MESH)

    for k in range(4):
        turned = meta_ref[pl.ds(8 * k, 8), :].T
        for j in range(KPAD // LANES):
            meta[pl.ds(j * LANES, LANES), k : k + 1] = turned[:, j : j + 1]
    lane = lax.broadcasted_iota(jnp.int32, (8, LANES), 1)
    cnt[...] = jnp.where(
        lane == 0,
        jnp.sum(jnp.sum(meta_ref[16:24, :], axis=0, keepdims=True), axis=1, keepdims=True),
        jnp.where(
            lane == 1,
            jnp.sum(jnp.sum(meta_ref[24:32, :], axis=0, keepdims=True), axis=1, keepdims=True),
            0.0,
        ),
    )
    sc[pl.ds(ROWS, KPAD - ROWS), :] = jnp.zeros((KPAD - ROWS, VW), jnp.bfloat16)
    loads[0].wait()
    for half in range(2):
        for (first, size), cols in zip(WHOLE, (slice(None), zc, slice(None))):
            rows = pl.ds(half * PIECE + first, size)
            wh[c, y, 2 * xh + half, pl.ds(first, size), cols] = w_ref[rows, cols].astype(
                jnp.bfloat16
            )
    pl.semaphore_wait(barrier, len(greeted))

    def count_start(stage, axis):
        return [
            send(cnt, cnt_in.at[stage, d - 1], peer(axis, d), "cnt", stage, d) for d in (1, 2, 3)
        ]

    def count_end(stage, copies):
        for copy in copies:
            copy.wait()
        total = cnt[...]
        for d in range(3):
            total = total + cnt_in[stage, d]
        cnt[...] = total

    def transpose_chunk(k):
        loads[1 + k].wait()

        def step(j, carry):
            cols = pl.ds(pl.multiple_of(k * 1280 + j * LANES, LANES), LANES)
            block = jnp.concatenate(
                [st[:, cols], jnp.zeros((KPAD - ROWS, LANES), jnp.bfloat16)], axis=0
            )
            st_t[cols, :] = block.T
            return carry

        lax.fori_loop(0, 10, step, 0)

    def fwd_chunk(yy, first):
        def step(i, carry):
            rows = pl.ds(pl.multiple_of(i * ROW_TILE, ROW_TILE), ROW_TILE)
            weight = jnp.concatenate(
                [
                    wh[core, yy, pl.ds(2 * half, 2)].reshape(2 * PIECE, VW)
                    for half in (0, 1)
                    for core in (0, 1)
                ],
                axis=0,
            )
            cols = pl.ds(pl.multiple_of(yy * 1280, 1280), 1280)
            proj = jnp.dot(st[rows, cols], weight, preferred_element_type=jnp.float32)
            prod = proj * f32(rd[rows, :])
            part = (
                prod[:, 0:128] + prod[:, 128:256] + prod[:, 256:384] + prod[:, 384:512]
            )
            if first:
                acc[rows, :] = part
            else:
                acc[rows, :] += part
            return carry

        lax.fori_loop(0, ROWS // ROW_TILE, step, 0)

    def scale_rows(u):
        total = jnp.maximum(cnt[0:1, u : u + 1], 1.0)

        def step(i, carry):
            rows = pl.ds(pl.multiple_of(i * ROW_TILE, ROW_TILE), ROW_TILE)
            shift, adv = meta[rows, 0:1], meta[rows, 1:2]
            weights = meta[rows, 2 + u : 3 + u]
            log_ratio = shift + jnp.sum(acc[rows, :], axis=1, keepdims=True)
            ratio = jnp.exp(log_ratio)
            clipped = jnp.clip(ratio, 1.0 - CLIP_EPS, 1.0 + CLIP_EPS)
            chosen = ratio * adv <= clipped * adv
            coeff = jnp.where(
                (weights > 0.0) & chosen, -(weights / total) * adv * ratio, 0.0
            )
            sc[rows, :] = (coeff * f32(rd[rows, :])).astype(jnp.bfloat16)
            return carry

        lax.fori_loop(0, ROWS // ROW_TILE, step, 0)

    def grad_block(core, yy, halves, first, height):
        blocks = []
        for half in halves:
            for low in (0, 1):
                start = yy * 1280 + half * 640 + core * 320 + low * PIECE + first
                blocks.append(st_t[pl.ds(pl.multiple_of(start, 16), height), :])
        product = jnp.dot(
            jnp.concatenate(blocks, axis=0), sc[...], preferred_element_type=jnp.float32
        )
        return product.reshape(len(blocks), height, VW)

    def add_up(own, parts):
        total = f32(own)
        for part in parts:
            total = total + f32(part)
        return total

    def share(u):
        block = out_ref.at[u, own_rows, zc]
        return [send(block, block, peer("z", d), "share", u, 0, d) for d in (1, 2, 3)] + [
            send(block, block, replicas[d], "share", u, 1, d) for d in range(4)
        ]

    class Gather:
        def __init__(self, name, parts):
            self.name = name
            self.rows = [pl.ds(first, size) for first, size in parts]
            self.sent, self.part_y, self.part_z, self.part_x = [], {}, {}, {}

        def ring(self, axis, block, *name, to=(1, 3, 2)):
            copies = {}
            for d in to:
                target = flipped[d] if axis == "x" else peer(axis, d)
                copies[d] = send(block, block, target, self.name, *name, d)
            self.sent.extend(copies.values())
            return copies

        def along_y(self, g):
            block = wh.at[c, y, flip[g], self.rows[0], :]
            self.part_y[g] = self.ring("y", block, "y", g, to=(1, 3))

        def along_z(self, o):
            block = wh.at[c, turn("y", o), :, self.rows[1], zc]
            self.part_z[o] = self.ring("z", block, "z", o)

        def along_x(self, o, to=(1, 3, 2)):
            block = wh.at[c, turn("y", o), x, self.rows[2], :]
            self.part_x[o] = self.ring("x", block, "x", o, to=to)

        def relay(self):
            self.relays = []
            for g, d in ((0, 1), (1, 3), (2, 1), (3, 3)):
                self.part_y[g][d].wait_recv()
                block = wh.at[c, turn("y", -d), flip[g], self.rows[0], :]
                self.relays.append(send(block, block, peer("y", d), self.name, "relay", g))
            self.sent += self.relays

        def arrived(self, o):
            if o == 2:
                for copy in self.relays:
                    copy.wait_recv()
            elif o:
                for g in range(4):
                    if (g, 4 - o) not in ((0, 1), (1, 3), (2, 1), (3, 3)):
                        self.part_y[g][4 - o].wait_recv()
            for copy in list(self.part_z[o].values()) + list(self.part_x[o].values()):
                copy.wait_recv()

    def gather_first(gather):
        second = gather.ring("x", wh.at[c, y, x, gather.rows[0], :], "ag2", 0, to=(3, 2))
        both = wh.at[c, y, pl.ds(2 * xh, 2), gather.rows[1], zc]
        plane = [send(both, both, across_xy[0], "ag2", 1, 0)]
        plane += [send(both, both, peer("y", d), "ag2", 1, 1, d) for d in (1, 2, 3)]
        plane += [send(both, both, across_xy[d], "ag2", 1, 2, d) for d in (1, 2, 3)]
        gather.sent += plane
        third = gather.ring("y", wh.at[c, y, x, gather.rows[2], :], "ag2", 2)
        gather.along_x(0, to=(3, 2))
        gather.along_y(0)
        gather.along_y(1)
        counting = count_start(0, "z")
        transpose_chunk(0)
        count_end(0, counting)
        counting = count_start(1, "x")
        for copy in plane:
            copy.wait_recv()
        gather.along_z(0)
        for g in (3, 2):
            second[g].wait_recv()
            gather.along_y(g)
        for o in (1, 3, 2):
            gather.along_z(o)
            third[4 - o].wait_recv()
            gather.along_x(o)
        transpose_chunk(1)
        count_end(1, counting)
        counting = count_start(2, "y")
        gather.relay()
        transpose_chunk(2)
        transpose_chunk(3)
        count_end(2, counting)
        return [send(cnt, cnt_in.at[3, 0], twin, "cnt", 3)]

    def gather_steps(gather):
        first = [
            gather.ring(axis, wh.at[c, y, x, gather.rows[p], zc], "ag1", p)
            for p, axis in enumerate("zxy")
        ]
        yield
        for copy in first[0].values():
            copy.wait_recv()
        second = [gather.ring("x", wh.at[c, y, x, gather.rows[0], :], "ag2", 0)]
        for copy in first[1].values():
            copy.wait_recv()
        second.append(gather.ring("y", wh.at[c, y, :, gather.rows[1], zc], "ag2", 1))
        for copy in first[2].values():
            copy.wait_recv()
        second.append(gather.ring("z", wh.at[c, :, x, gather.rows[2], zc], "ag2", 2))
        gather.along_y(0)
        gather.along_z(0)
        yield
        for g in (1, 3):
            second[0][g].wait_recv()
            gather.along_y(g)
        for copy in second[2].values():
            copy.wait_recv()
        gather.along_x(0)
        second[0][2].wait_recv()
        gather.along_y(2)
        for o in (1, 3, 2):
            second[1][4 - o].wait_recv()
            gather.along_z(o)
            gather.along_x(o)
        yield
        gather.relay()
        yield

    def reduce_steps(u, h, given, sent):
        kind, parts = SUM_TYPES[u], STREAMS[u][h]
        base, height = parts[0][0], sum(size for _, size in parts)
        rows = [pl.ds(first - base, size) for first, size in parts]
        at = N_SUMS * (h if u == 0 else len(STREAMS[0]))
        gsend, gs, rel, r0, r1, r2, s0, s1, s2, q0, q1, q2, total = sums[at : at + N_SUMS]
        groups = ((0, 1),) if height < PIECE else ((0,), (1,))
        outs, relayed, hop = {}, [], []

        def give(i):
            yy = turn("y", CHUNKS_OUT[i])
            if i >= 2:
                given[-2].wait_send()
            for halves in groups:
                gsend[i % 2, pl.ds(2 * halves[0], 2 * len(halves))] = grad_block(
                    1 - c, yy, halves, base, height
                ).astype(kind)
            given.append(send(gsend.at[i % 2], gs.at[yy], twin, "rsc", h, i))
            return given[-1]

        def keep(i):
            yy = turn("y", CHUNKS_OUT[i])
            gifts[i].wait_recv()
            for halves in groups:
                these = pl.ds(2 * halves[0], 2 * len(halves))
                gs[yy, these] = (
                    grad_block(c, yy, halves, base, height) + f32(gs[yy, these])
                ).astype(kind)

        def first_sends(o):
            yy = turn("y", o)
            for d in (2, 1, 3):
                outs[1, o, d] = send(
                    gs.at[yy, :, rows[1], lanes(turn("z", d))], r1.at[d - 1, yy],
                    peer("z", d), "rs1", h, 1, o, d,
                )
                outs[2, o, d] = send(
                    gs.at[yy, turn("x", d), rows[2], :], r2.at[d - 1, yy],
                    peer("x", d), "rs1", h, 2, o, d,
                )

        def first_sums(o):
            yy = turn("y", o)
            for d in (1, 2, 3):
                outs[1, o, d].wait_recv()
            s1[yy] = add_up(gs[yy, :, rows[1], zc], [r1[d, yy] for d in range(3)]).astype(kind)
            for d in (2, 1, 3, 0):
                if o or d:
                    xx = turn("x", d)
                    hop.append(
                        send(
                            s1.at[yy, xx], q1.at[o, d], device(xx, yy, z, c),
                            "rs2", h, 1, o, d,
                        )
                    )
            for d in (1, 2, 3):
                outs[2, o, d].wait_recv()
            s2[yy] = add_up(gs[yy, x, rows[2], :], [r2[d, yy] for d in range(3)]).astype(kind)
            for d in (2, 1, 3, 0):
                if o or d:
                    zz = turn("z", d)
                    hop.append(
                        send(
                            s2.at[yy, :, lanes(zz)], q2.at[o, d], device(x, yy, zz, c),
                            "rs2", h, 2, o, d,
                        )
                    )

        def pass_on(o):
            yy = turn("y", o)
            side = 0 if o == 1 else 1
            relayed[side].wait_recv()
            for k in range(2):
                gs[yy, 2 * side + k, rows[0], :] = (
                    f32(gs[yy, 2 * side + k, rows[0], :]) + f32(rel[side, k])
                ).astype(kind)
            outs[0, o, 0] = send(
                gs.at[yy, :, rows[0], :], r0.at[side], peer("y", o), "rs1", h, 0, o
            )

        gifts = [give(0)]
        for i, o in enumerate(CHUNKS_OUT):
            if i + 1 < 4:
                gifts.append(give(i + 1))
            keep(i)
            if i == 0:
                relayed += [
                    send(
                        gs.at[turn("y", 2), pl.ds(2 * side, 2), rows[0], :], rel.at[side],
                        peer("y", 1 + 2 * side), "rs0", h, side,
                    )
                    for side in range(2)
                ]
            first_sends(o)
            if i >= 2:
                pass_on(CHUNKS_OUT[i - 1])
            if i:
                first_sums(CHUNKS_OUT[i - 1])
            yield
        for o in (1, 3):
            outs[0, o, 0].wait_recv()
        for d in (2, 1, 3, 0):
            xx = turn("x", d)
            s0[xx] = add_up(gs[y, xx, rows[0], :], [r0[0, xx], r0[1, xx]]).astype(kind)
            for e in (2, 1, 3, 0):
                if d or e:
                    zz = turn("z", e)
                    hop.append(
                        send(
                            s0.at[xx, :, lanes(zz)], q0.at[d, e], device(xx, y, zz, c),
                            "rs2", h, 0, d, e,
                        )
                    )
        first_sums(CHUNKS_OUT[3])
        yield
        for copy in hop:
            copy.wait_recv()
        others = [(d, e) for d in range(4) for e in range(4) if d or e]
        owns = (s0[x, :, zc], s1[y, x], s2[y, :, zc])
        for p, got in enumerate((q0, q1, q2)):
            total[rows[p], :] = add_up(owns[p], [got[d, e] for d, e in others])
        gradient = total[...]
        out_ref[u, pl.ds(pl.multiple_of(xl * PIECE + base, 16), height), zc] = gradient.astype(
            jnp.bfloat16
        )
        if u == 0:
            if h == 0:
                for load in loads[6:]:
                    load.wait()
            these = pl.ds(base, height)
            master, _, _ = adam_step(
                w_ref[pl.ds(pl.multiple_of(xl * PIECE + base, 16), height), zc],
                m_ref[these, :], v_ref[these, :], gradient, PRIOR_STEPS + 1,
            )
            wh[c, y, x, these, zc] = master.astype(jnp.bfloat16)
        sent += relayed + gifts[2:] + list(outs.values()) + hop

    def stream_steps(h, gather, given, sent):
        yield from reduce_steps(0, h, given, sent)
        yield from gather_steps(gather)

    def multiply(u, gathers, shared):
        across = {}
        for i, o in enumerate(CHUNKS_IN):
            for a in CHUNKS_IN[:2] if i == 0 else CHUNKS_IN[i + 1 : i + 2]:
                for gather in gathers:
                    gather.arrived(a)
                block = wh.at[c, turn("y", a)]
                across[a] = send(block, block, twin, "agc", a)
                if u == 1 and a == CHUNKS_IN[3]:
                    shared += share(0)
            across[o].wait_recv()
            fwd_chunk(turn("y", o), i == 0)
        return list(across.values())

    shared = []
    gathers = [Gather("w0", WHOLE)]
    counting = gather_first(gathers[0])
    loads[5].wait()
    sent = multiply(0, gathers, shared)
    counting[0].wait()
    cnt[...] = cnt[...] + cnt_in[3, 0]
    scale_rows(0)
    for copy in sent + gathers[0].sent:
        copy.wait_send()

    sent, given = [], []
    gathers = [Gather("w1" + "ab"[h], parts) for h, parts in enumerate(STREAMS[0])]
    ahead, behind = [stream_steps(h, gathers[h], given, sent) for h in range(2)]
    for _ in range(4):
        next(ahead)
    running = [behind, ahead]
    while running:
        running = [steps for steps in running if next(steps, running) is not running]
    sent += multiply(1, gathers, shared)
    scale_rows(1)
    for copy in sent + gathers[0].sent + gathers[1].sent:
        copy.wait_send()

    sent = []
    for _ in reduce_steps(1, 0, [], sent):
        pass
    shared += share(1)
    for copy in shared:
        copy.wait_recv()
    for copy in sent + shared:
        copy.wait_send()


def body(
    states, readout, logp_shift, advantage, response_mask, rollout_len, dest_slot,
    weight, moment1, moment2,
):
    row_index = jnp.arange(ROWS, dtype=jnp.int32)
    live = (row_index < rollout_len[0]) & (dest_slot >= 0)
    batch = jnp.where(live, (dest_slot % BAL) // MB, UPDATES)
    token = response_mask.astype(jnp.float32)
    lines = [logp_shift.astype(jnp.float32), advantage.astype(jnp.float32)]
    lines += [jnp.where(batch == k, token, 0.0) for k in range(UPDATES)]
    meta = jnp.concatenate([jnp.pad(line, (0, 1024 - ROWS)) for line in lines])
    meta = meta.reshape(4 * 8, LANES)
    bf16, full = jnp.bfloat16, jnp.float32
    vmem = pl.BlockSpec(memory_space=pltpu.VMEM)
    hbm = pl.BlockSpec(memory_space=pl.ANY)
    sums = []
    for kind, streams in zip(SUM_TYPES, STREAMS):
        for parts in streams:
            *parcels, total = sums_of(parts)
            sums += [pltpu.VMEM(dims, kind) for dims in parcels] + [pltpu.VMEM(total, full)]
    gradients = pl.pallas_call(
        kernel,
        out_shape=jax.ShapeDtypeStruct((UPDATES,) + weight.shape, bf16),
        in_specs=[hbm, hbm, vmem, hbm, hbm, hbm],
        out_specs=vmem,
        scratch_shapes=[
            pltpu.VMEM((ROWS, D), bf16),
            pltpu.VMEM((D, KPAD), bf16),
            pltpu.VMEM((ROWS, VW), bf16),
            pltpu.VMEM((KPAD, 8), full),
            pltpu.VMEM((2 * PIECE, VW), full),
            pltpu.VMEM((PIECE, LANES), full),
            pltpu.VMEM((PIECE, LANES), full),
            pltpu.VMEM((2, 4, 4, PIECE, VW), bf16),
            pltpu.VMEM((ROWS, LANES), full),
            pltpu.VMEM((KPAD, VW), bf16),
            pltpu.VMEM((8, LANES), full),
            pltpu.VMEM((4, 3, 8, LANES), full),
            pltpu.SemaphoreType.DMA((8,)),
            pltpu.SemaphoreType.DMA((N_SEMS,)),
            pltpu.SemaphoreType.DMA((N_SEMS,)),
        ]
        + sums,
        compiler_params=pltpu.CompilerParams(
            collective_id=0, has_side_effects=True, vmem_limit_bytes=58 * 1024 * 1024
        ),
    )(states, readout, meta, weight, moment1, moment2)
    master, one, two = weight, moment1, moment2
    for u in range(UPDATES):
        master, one, two = adam_step(
            master, one, two, gradients[u].astype(full), PRIOR_STEPS + u + 1
        )
    return master, one, two


def solution(mesh):
    rows = P(("dp", "shard"))
    return jax.shard_map(
        body,
        mesh=mesh,
        in_specs=(
            P(("dp", "shard"), None), P(("dp", "shard"), None), rows, rows, rows, rows, rows,
            P("shard", None), P("shard", None), P("shard", None),
        ),
        out_specs=(P("shard", None), P("shard", None), P("shard", None)),
        check_vma=False,
    )
```

```python
import jax
import jax.numpy as jnp
from jax import lax
from jax.experimental import pallas as pl
from jax.experimental.pallas import tpu as pltpu
from jax.sharding import PartitionSpec as P

MESH = pl.DeviceIdType.MESH

BAL = 576
UPDATES = 2
PRIOR_STEPS = 100
MB = 288
ROWS = 864
KPAD = 896
D = 5120
VW = 512
PIECE = 160
LANES = 128
ROW_TILE = 288

BETA_ONE = 0.9
BETA_TWO = 0.999
LEARN_RATE = 0.001
DECAY_RATE = 0.01
ADAM_EPS = 1e-08
CLIP_EPS = 0.2

WHOLE = ((0, 64), (64, 48), (112, 48))
STREAMS = (
    (WHOLE,),
    (WHOLE,),
)
SUM_TYPES = (jnp.float32, jnp.bfloat16)
CHUNKS_IN = (0, 1, 3, 2)
CHUNKS_OUT = (2, 1, 3, 0)


def adam_step(master, moment_one, moment_two, gradient, step_num):
    moment_one = BETA_ONE * moment_one + (1.0 - BETA_ONE) * gradient
    moment_two = BETA_TWO * moment_two + (1.0 - BETA_TWO) * gradient * gradient
    first_hat = moment_one / (1.0 - BETA_ONE**step_num)
    second_hat = moment_two / (1.0 - BETA_TWO**step_num)
    master = master - LEARN_RATE * (
        first_hat / (jnp.sqrt(second_hat) + ADAM_EPS) + DECAY_RATE * master
    )
    return (master, moment_one, moment_two)


class Sems:
    def __init__(self, send, recv):
        self.send, self.recv, self.index = send, recv, {}

    def pair(self, *name):
        slot = self.index.setdefault(name, len(self.index))
        return self.send.at[slot], self.recv.at[slot]


N_SEMS = 400
RELAY_BY = (1, 3, 1, 3)
N_SUMS = 13


def sums_of(parts):
    (_, a), (_, b), (_, d) = parts
    height = a + b + d
    return [
        (2, 4, height, VW), (4, 4, height, VW), (2, 2, a, VW),
        (2, 4, a, VW), (3, 4, 4, b, LANES), (3, 4, d, VW),
        (4, a, VW), (4, 4, b, LANES), (4, d, VW),
        (4, 4, a, LANES), (4, 4, b, LANES), (4, 4, d, LANES),
        (height, LANES),
    ]


def f32(value):
    return value.astype(jnp.float32)


def kernel(
    states_hbm, read_hbm, shift_ref, adv_ref, mask_ref, len_ref, slot_ref, w_hbm, m_hbm, v_hbm,
    out_ref,
    st, st_t, rd, meta, w_ref, m_ref, v_ref, wh, acc, sc, cnt, cnt_in,
    load_sem, send_sem, recv_sem, *sums,
):
    dp, sh = lax.axis_index("dp"), lax.axis_index("shard")
    xl, z = dp // 4, dp % 4
    y, xh, c = sh // 4, (sh // 2) % 2, sh % 2
    x = xh * 2 + xl

    def device(x_, y_, z_, c_):
        return ((x_ % 2) * 4 + z_, y_ * 4 + (x_ // 2) * 2 + c_)

    def turn(axis, d):
        return ({"x": x, "y": y, "z": z}[axis] + d) % 4

    def peer(axis, d):
        to = turn(axis, d)
        return device(
            to if axis == "x" else x, to if axis == "y" else y, to if axis == "z" else z, c
        )

    twin = device(x, y, z, 1 - c)
    pair = xh * 2 + (1 - xl)
    replicas = [device(pair, y, turn("z", d), c) for d in range(4)]
    across_xy = [device(turn("x", 2), turn("y", d), z, c) for d in range(4)]
    flip = (x, pair, turn("x", 2), 3 - x)
    flipped = [device(to, y, z, c) for to in flip]

    def lanes(index):
        return pl.ds(pl.multiple_of(index * LANES, LANES), LANES)

    zc = lanes(z)
    sems = Sems(send_sem, recv_sem)

    def send(src, dst, to, *name):
        send_at, recv_at = sems.pair(*name)
        copy = pltpu.make_async_remote_copy(
            src_ref=src, dst_ref=dst, send_sem=send_at, recv_sem=recv_at,
            device_id=to, device_id_type=MESH,
        )
        copy.start()
        return copy

    own_rows = pl.ds(pl.multiple_of(xl * PIECE, PIECE), PIECE)

    loads = [pltpu.make_async_copy(w_hbm, w_ref, load_sem.at[0])]
    for k in range(4):
        cols = pl.ds(k * 1280, 1280)
        loads.append(
            pltpu.make_async_copy(states_hbm.at[:, cols], st.at[:, cols], load_sem.at[1 + k])
        )
    loads.append(pltpu.make_async_copy(read_hbm, rd, load_sem.at[5]))
    loads.append(pltpu.make_async_copy(m_hbm.at[own_rows, zc], m_ref, load_sem.at[6]))
    loads.append(pltpu.make_async_copy(v_hbm.at[own_rows, zc], v_ref, load_sem.at[7]))
    for load in loads:
        load.start()

    barrier = pltpu.get_barrier_semaphore()
    greeted = [peer(axis, d) for axis in "xyz" for d in (1, 2, 3)] + [twin]
    greeted += replicas[1:] + across_xy[1:]
    for to in greeted:
        pl.semaphore_signal(barrier, inc=1, device_id=to, device_id_type=MESH)

    loads[0].wait()
    for half in range(2):
        for (first, size), cols in zip(WHOLE, (slice(None), zc, slice(None))):
            rows = pl.ds(half * PIECE + first, size)
            wh[c, y, 2 * xh + half, pl.ds(first, size), cols] = w_ref[rows, cols].astype(
                jnp.bfloat16
            )
    pl.semaphore_wait(barrier, len(greeted))

    def prepare():
        def line(ref):
            row = f32(ref[...]).reshape(1, ROWS)
            return jnp.concatenate([row, jnp.zeros((1, KPAD - ROWS), jnp.float32)], axis=1)

        slot = line(slot_ref)
        place = lax.broadcasted_iota(jnp.int32, (1, KPAD), 1)
        live = (place < len_ref[0]) & (slot >= 0.0) & (place < ROWS)
        batch = jnp.floor((slot + 0.5) * (1.0 / MB))
        odd = batch - 2.0 * jnp.floor(batch * 0.5)
        token = jnp.where(live, line(mask_ref), 0.0)
        tokens = [jnp.where(odd < 0.5, token, 0.0), jnp.where(odd < 0.5, 0.0, token)]
        lines = [line(shift_ref), line(adv_ref)] + tokens
        meta[...] = jnp.concatenate(lines + [jnp.zeros((4, KPAD), jnp.float32)], axis=0).T
        lane = lax.broadcasted_iota(jnp.int32, (8, LANES), 1)
        sums_now = [jnp.sum(row, axis=1, keepdims=True) for row in tokens]
        cnt[...] = jnp.where(lane == 0, sums_now[0], jnp.where(lane == 1, sums_now[1], 0.0))
        sc[pl.ds(ROWS, KPAD - ROWS), :] = jnp.zeros((KPAD - ROWS, VW), jnp.bfloat16)

    def count_start(stage, axis):
        return [
            send(cnt, cnt_in.at[stage, d - 1], peer(axis, d), "cnt", stage, d) for d in (1, 2, 3)
        ]

    def count_end(stage, copies):
        for copy in copies:
            copy.wait()
        total = cnt[...]
        for d in range(3):
            total = total + cnt_in[stage, d]
        cnt[...] = total

    def transpose_chunk(k):
        loads[1 + k].wait()

        def step(j, carry):
            cols = pl.ds(pl.multiple_of(k * 1280 + j * LANES, LANES), LANES)
            block = jnp.concatenate(
                [st[:, cols], jnp.zeros((KPAD - ROWS, LANES), jnp.bfloat16)], axis=0
            )
            st_t[cols, :] = block.T
            return carry

        lax.fori_loop(0, 10, step, 0)

    def fwd_chunk(yy, first):
        def step(i, carry):
            rows = pl.ds(pl.multiple_of(i * ROW_TILE, ROW_TILE), ROW_TILE)
            weight = jnp.concatenate(
                [
                    wh[core, yy, pl.ds(2 * half, 2)].reshape(2 * PIECE, VW)
                    for half in (0, 1)
                    for core in (0, 1)
                ],
                axis=0,
            )
            cols = pl.ds(pl.multiple_of(yy * 1280, 1280), 1280)
            proj = jnp.dot(st[rows, cols], weight, preferred_element_type=jnp.float32)
            prod = proj * f32(rd[rows, :])
            part = (
                prod[:, 0:128] + prod[:, 128:256] + prod[:, 256:384] + prod[:, 384:512]
            )
            if first:
                acc[rows, :] = part
            else:
                acc[rows, :] += part
            return carry

        lax.fori_loop(0, ROWS // ROW_TILE, step, 0)

    def scale_rows(u):
        total = jnp.maximum(cnt[0:1, u : u + 1], 1.0)

        def step(i, carry):
            rows = pl.ds(pl.multiple_of(i * ROW_TILE, ROW_TILE), ROW_TILE)
            shift, adv = meta[rows, 0:1], meta[rows, 1:2]
            weights = meta[rows, 2 + u : 3 + u]
            log_ratio = shift + jnp.sum(acc[rows, :], axis=1, keepdims=True)
            ratio = jnp.exp(log_ratio)
            clipped = jnp.clip(ratio, 1.0 - CLIP_EPS, 1.0 + CLIP_EPS)
            chosen = ratio * adv <= clipped * adv
            coeff = jnp.where(
                (weights > 0.0) & chosen, -(weights / total) * adv * ratio, 0.0
            )
            sc[rows, :] = (coeff * f32(rd[rows, :])).astype(jnp.bfloat16)
            return carry

        lax.fori_loop(0, ROWS // ROW_TILE, step, 0)

    def grad_block(core, yy, halves, first, height):
        blocks = []
        for half in halves:
            for low in (0, 1):
                start = yy * 1280 + half * 640 + core * 320 + low * PIECE + first
                blocks.append(st_t[pl.ds(pl.multiple_of(start, 16), height), :])
        product = jnp.dot(
            jnp.concatenate(blocks, axis=0), sc[...], preferred_element_type=jnp.float32
        )
        return product.reshape(len(blocks), height, VW)

    def add_up(own, parts):
        total = f32(own)
        for part in parts:
            total = total + f32(part)
        return total

    def share(u):
        block = out_ref.at[u, own_rows, zc]
        return [send(block, block, peer("z", d), "share", u, 0, d) for d in (1, 2, 3)] + [
            send(block, block, replicas[d], "share", u, 1, d) for d in range(4)
        ]

    class Gather:
        def __init__(self, name, parts):
            self.name = name
            self.rows = [pl.ds(first, size) for first, size in parts]
            self.sent, self.part_y, self.part_z, self.part_x = [], {}, {}, {}
            self.relays = []

        def ring(self, axis, block, *name, to=(1, 3, 2)):
            copies = {}
            for d in to:
                target = flipped[d] if axis == "x" else peer(axis, d)
                copies[d] = send(block, block, target, self.name, *name, d)
            self.sent.extend(copies.values())
            return copies

        def along_y(self, g):
            block = wh.at[c, y, flip[g], self.rows[0], :]
            self.part_y[g] = self.ring("y", block, "y", g, to=(1, 3))

        def along_z(self, o):
            block = wh.at[c, turn("y", o), :, self.rows[1], zc]
            self.part_z[o] = self.ring("z", block, "z", o)

        def along_x(self, o, to=(1, 3, 2)):
            block = wh.at[c, turn("y", o), x, self.rows[2], :]
            self.part_x[o] = self.ring("x", block, "x", o, to=to)

        def relay(self, *blocks):
            for g in blocks:
                d = RELAY_BY[g]
                self.part_y[g][d].wait_recv()
                block = wh.at[c, turn("y", -d), flip[g], self.rows[0], :]
                self.relays.append(send(block, block, peer("y", d), self.name, "relay", g))

        def arrived(self, o):
            if o == 2:
                for copy in self.relays:
                    copy.wait_recv()
            elif o:
                for g in range(4):
                    if RELAY_BY[g] != 4 - o:
                        self.part_y[g][4 - o].wait_recv()
            for copy in list(self.part_z[o].values()) + list(self.part_x[o].values()):
                copy.wait_recv()

    def gather_first(gather):
        second = gather.ring("x", wh.at[c, y, x, gather.rows[0], :], "ag2", 0, to=(3, 2))
        both = wh.at[c, y, pl.ds(2 * xh, 2), gather.rows[1], zc]
        plane = [send(both, both, across_xy[0], "ag2", 1, 0)]
        plane += [send(both, both, peer("y", d), "ag2", 1, 1, d) for d in (1, 2, 3)]
        plane += [send(both, both, across_xy[d], "ag2", 1, 2, d) for d in (1, 2, 3)]
        gather.sent += plane
        third = gather.ring("y", wh.at[c, y, x, gather.rows[2], :], "ag2", 2)
        gather.along_x(0, to=(3, 2))
        gather.along_y(0)
        gather.along_y(1)
        prepare()
        counting = count_start(0, "z")
        transpose_chunk(0)
        count_end(0, counting)
        counting = count_start(1, "x")
        for copy in plane:
            copy.wait_recv()
        gather.along_z(0)
        for g in (3, 2):
            second[g].wait_recv()
            gather.along_y(g)
        for o in (1, 3, 2):
            gather.along_z(o)
            third[4 - o].wait_recv()
            gather.along_x(o)

        def between():
            gather.relay(0, 1)
            transpose_chunk(1)
            count_end(1, counting)
            counting_y = count_start(2, "y")
            gather.relay(2, 3)
            transpose_chunk(2)
            transpose_chunk(3)
            count_end(2, counting_y)
            loads[5].wait()

        return between

    def gather_steps(gather):
        first = [
            gather.ring(axis, wh.at[c, y, x, gather.rows[p], zc], "ag1", p)
            for p, axis in enumerate("zxy")
        ]
        yield
        for copy in first[0].values():
            copy.wait_recv()
        second = [gather.ring("x", wh.at[c, y, x, gather.rows[0], :], "ag2", 0)]
        for copy in first[1].values():
            copy.wait_recv()
        second.append(gather.ring("y", wh.at[c, y, :, gather.rows[1], zc], "ag2", 1))
        for copy in first[2].values():
            copy.wait_recv()
        second.append(gather.ring("z", wh.at[c, :, x, gather.rows[2], zc], "ag2", 2))
        gather.along_y(0)
        gather.along_z(0)
        yield
        for g in (1, 3):
            second[0][g].wait_recv()
            gather.along_y(g)
        for copy in second[2].values():
            copy.wait_recv()
        gather.along_x(0)
        second[0][2].wait_recv()
        gather.along_y(2)
        for o in (1, 3, 2):
            second[1][4 - o].wait_recv()
            gather.along_z(o)
            gather.along_x(o)
        yield
        gather.relay(0, 1)

    def reduce_steps(u, h, given, sent):
        kind, parts = SUM_TYPES[u], STREAMS[u][h]
        base, height = parts[0][0], sum(size for _, size in parts)
        rows = [pl.ds(first - base, size) for first, size in parts]
        at = N_SUMS * (h if u == 0 else len(STREAMS[0]))
        gsend, gs, rel, r0, r1, r2, s0, s1, s2, q0, q1, q2, total = sums[at : at + N_SUMS]
        groups = ((0, 1),) if height < PIECE else ((0,), (1,))
        outs, relayed, hop = {}, [], []

        def give(i):
            yy = turn("y", CHUNKS_OUT[i])
            if i >= 2:
                given[-2].wait_send()
            for halves in groups:
                gsend[i % 2, pl.ds(2 * halves[0], 2 * len(halves))] = grad_block(
                    1 - c, yy, halves, base, height
                ).astype(kind)
            given.append(send(gsend.at[i % 2], gs.at[yy], twin, "rsc", h, i))
            return given[-1]

        def keep(i):
            yy = turn("y", CHUNKS_OUT[i])
            gifts[i].wait_recv()
            for halves in groups:
                these = pl.ds(2 * halves[0], 2 * len(halves))
                gs[yy, these] = (
                    grad_block(c, yy, halves, base, height) + f32(gs[yy, these])
                ).astype(kind)

        def first_sends(o):
            yy = turn("y", o)
            for d in (2, 1, 3):
                outs[1, o, d] = send(
                    gs.at[yy, :, rows[1], lanes(turn("z", d))], r1.at[d - 1, yy],
                    peer("z", d), "rs1", h, 1, o, d,
                )
                outs[2, o, d] = send(
                    gs.at[yy, turn("x", d), rows[2], :], r2.at[d - 1, yy],
                    peer("x", d), "rs1", h, 2, o, d,
                )

        def first_sums(o):
            yy = turn("y", o)
            for d in (1, 2, 3):
                outs[1, o, d].wait_recv()
            s1[yy] = add_up(gs[yy, :, rows[1], zc], [r1[d, yy] for d in range(3)]).astype(kind)
            for d in (2, 1, 3, 0):
                if o or d:
                    xx = turn("x", d)
                    hop.append(
                        send(
                            s1.at[yy, xx], q1.at[o, d], device(xx, yy, z, c),
                            "rs2", h, 1, o, d,
                        )
                    )
            for d in (1, 2, 3):
                outs[2, o, d].wait_recv()
            s2[yy] = add_up(gs[yy, x, rows[2], :], [r2[d, yy] for d in range(3)]).astype(kind)
            for d in (2, 1, 3, 0):
                if o or d:
                    zz = turn("z", d)
                    hop.append(
                        send(
                            s2.at[yy, :, lanes(zz)], q2.at[o, d], device(x, yy, zz, c),
                            "rs2", h, 2, o, d,
                        )
                    )

        def pass_on(o):
            yy = turn("y", o)
            side = 0 if o == 1 else 1
            relayed[side].wait_recv()
            for k in range(2):
                gs[yy, 2 * side + k, rows[0], :] = (
                    f32(gs[yy, 2 * side + k, rows[0], :]) + f32(rel[side, k])
                ).astype(kind)
            outs[0, o, 0] = send(
                gs.at[yy, :, rows[0], :], r0.at[side], peer("y", o), "rs1", h, 0, o
            )

        gifts = [give(0)]
        for i, o in enumerate(CHUNKS_OUT):
            if i + 1 < 4:
                gifts.append(give(i + 1))
            keep(i)
            if i == 0:
                relayed += [
                    send(
                        gs.at[turn("y", 2), pl.ds(2 * side, 2), rows[0], :], rel.at[side],
                        peer("y", 1 + 2 * side), "rs0", h, side,
                    )
                    for side in range(2)
                ]
            first_sends(o)
            if i == 2:
                pass_on(CHUNKS_OUT[1])
                pass_on(CHUNKS_OUT[2])
            yield
        first_sums(CHUNKS_OUT[0])
        first_sums(CHUNKS_OUT[1])
        yield
        for o in (1, 3):
            outs[0, o, 0].wait_recv()
        for d in (2, 1, 3, 0):
            xx = turn("x", d)
            s0[xx] = add_up(gs[y, xx, rows[0], :], [r0[0, xx], r0[1, xx]]).astype(kind)
            for e in (2, 1, 3, 0):
                if d or e:
                    zz = turn("z", e)
                    hop.append(
                        send(
                            s0.at[xx, :, lanes(zz)], q0.at[d, e], device(xx, y, zz, c),
                            "rs2", h, 0, d, e,
                        )
                    )
        first_sums(CHUNKS_OUT[2])
        first_sums(CHUNKS_OUT[3])
        yield
        for copy in hop:
            copy.wait_recv()
        others = [(d, e) for d in range(4) for e in range(4) if d or e]
        owns = (s0[x, :, zc], s1[y, x], s2[y, :, zc])
        for p, got in enumerate((q0, q1, q2)):
            total[rows[p], :] = add_up(owns[p], [got[d, e] for d, e in others])
        gradient = total[...]
        out_ref[u, pl.ds(pl.multiple_of(xl * PIECE + base, 16), height), zc] = gradient.astype(
            jnp.bfloat16
        )
        if u == 0:
            if h == 0:
                for load in loads[6:]:
                    load.wait()
            these = pl.ds(base, height)
            master, _, _ = adam_step(
                w_ref[pl.ds(pl.multiple_of(xl * PIECE + base, 16), height), zc],
                m_ref[these, :], v_ref[these, :], gradient, PRIOR_STEPS + 1,
            )
            wh[c, y, x, these, zc] = master.astype(jnp.bfloat16)
        sent += relayed + gifts[2:] + list(outs.values()) + hop

    def stream_steps(h, gather, given, sent):
        yield from reduce_steps(0, h, given, sent)
        yield from gather_steps(gather)

    def multiply(gathers, between, before_last):
        across = {}

        def cross(o):
            for gather in gathers:
                gather.arrived(o)
            block = wh.at[c, turn("y", o)]
            across[o] = send(block, block, twin, "agc", o)

        cross(CHUNKS_IN[0])
        between()
        for i, o in enumerate(CHUNKS_IN):
            if i < 3:
                cross(CHUNKS_IN[i + 1])
            if i == 2:
                before_last()
            across[o].wait_recv()
            fwd_chunk(turn("y", o), i == 0)
        return list(across.values()) + [copy for gather in gathers for copy in gather.sent + gather.relays]

    shared, counting = [], []
    gathers = [Gather("w0", WHOLE)]
    between = gather_first(gathers[0])
    sent = multiply(
        gathers, between, lambda: counting.append(send(cnt, cnt_in.at[3, 0], twin, "cnt", 3))
    )
    counting[0].wait()
    cnt[...] = cnt[...] + cnt_in[3, 0]
    scale_rows(0)
    for copy in sent:
        copy.wait_send()

    sent, given = [], []
    gathers = [Gather("w1" + "ab"[h], parts) for h, parts in enumerate(STREAMS[0])]
    running = [stream_steps(h, gathers[h], given, sent) for h in range(len(gathers))]
    for _ in range(4):
        next(running[0])
    running = running[::-1]
    while running:
        running = [steps for steps in running if next(steps, running) is not running]
    sent += multiply(
        gathers,
        lambda: [gather.relay(2, 3) for gather in gathers],
        lambda: shared.extend(share(0)),
    )
    scale_rows(1)
    for copy in sent:
        copy.wait_send()

    sent = []
    for _ in reduce_steps(1, 0, [], sent):
        pass
    shared += share(1)
    for copy in shared:
        copy.wait_recv()
    for copy in sent + shared:
        copy.wait_send()


def body(
    states, readout, logp_shift, advantage, response_mask, rollout_len, dest_slot,
    weight, moment1, moment2,
):
    bf16, full = jnp.bfloat16, jnp.float32
    vmem = pl.BlockSpec(memory_space=pltpu.VMEM)
    hbm = pl.BlockSpec(memory_space=pl.ANY)
    smem = pl.BlockSpec(memory_space=pltpu.SMEM)
    sums = []
    for kind, streams in zip(SUM_TYPES, STREAMS):
        for parts in streams:
            *parcels, total = sums_of(parts)
            sums += [pltpu.VMEM(dims, kind) for dims in parcels] + [pltpu.VMEM(total, full)]
    gradients = pl.pallas_call(
        kernel,
        out_shape=jax.ShapeDtypeStruct((UPDATES,) + weight.shape, bf16),
        in_specs=[hbm, hbm, vmem, vmem, vmem, smem, vmem, hbm, hbm, hbm],
        out_specs=vmem,
        scratch_shapes=[
            pltpu.VMEM((ROWS, D), bf16),
            pltpu.VMEM((D, KPAD), bf16),
            pltpu.VMEM((ROWS, VW), bf16),
            pltpu.VMEM((KPAD, 8), full),
            pltpu.VMEM((2 * PIECE, VW), full),
            pltpu.VMEM((PIECE, LANES), full),
            pltpu.VMEM((PIECE, LANES), full),
            pltpu.VMEM((2, 4, 4, PIECE, VW), bf16),
            pltpu.VMEM((ROWS, LANES), full),
            pltpu.VMEM((KPAD, VW), bf16),
            pltpu.VMEM((8, LANES), full),
            pltpu.VMEM((4, 3, 8, LANES), full),
            pltpu.SemaphoreType.DMA((8,)),
            pltpu.SemaphoreType.DMA((N_SEMS,)),
            pltpu.SemaphoreType.DMA((N_SEMS,)),
        ]
        + sums,
        compiler_params=pltpu.CompilerParams(
            collective_id=0, has_side_effects=True, vmem_limit_bytes=58 * 1024 * 1024
        ),
    )(
        states, readout, logp_shift, advantage, response_mask, rollout_len, dest_slot,
        weight, moment1, moment2,
    )
    master, one, two = weight, moment1, moment2
    for u in range(UPDATES):
        master, one, two = adam_step(
            master, one, two, gradients[u].astype(full), PRIOR_STEPS + u + 1
        )
    return master, one, two


def solution(mesh):
    rows = P(("dp", "shard"))
    return jax.shard_map(
        body,
        mesh=mesh,
        in_specs=(
            P(("dp", "shard"), None), P(("dp", "shard"), None), rows, rows, rows, rows, rows,
            P("shard", None), P("shard", None), P("shard", None),
        ),
        out_specs=(P("shard", None), P("shard", None), P("shard", None)),
        check_vma=False,
    )
```

```python
import jax
import jax.numpy as jnp
from jax import lax
from jax.experimental import pallas as pl
from jax.experimental.pallas import tpu as pltpu
from jax.sharding import PartitionSpec as P

MESH = pl.DeviceIdType.MESH

BAL = 576
UPDATES = 2
PRIOR_STEPS = 100
MB = 288
ROWS = 864
KPAD = 896
D = 5120
VW = 512
PIECE = 160
LANES = 128
ROW_TILE = 288

BETA_ONE = 0.9
BETA_TWO = 0.999
LEARN_RATE = 0.001
DECAY_RATE = 0.01
ADAM_EPS = 1e-08
CLIP_EPS = 0.2

WHOLE = ((0, 64), (64, 48), (112, 48))
STREAMS = (
    (WHOLE,),
    (WHOLE,),
)
SUM_TYPES = (jnp.float32, jnp.bfloat16)
CHUNKS_IN = (0, 1, 3, 2)
CHUNKS_OUT = (2, 1, 3, 0)


def adam_step(master, moment_one, moment_two, gradient, step_num):
    moment_one = BETA_ONE * moment_one + (1.0 - BETA_ONE) * gradient
    moment_two = BETA_TWO * moment_two + (1.0 - BETA_TWO) * gradient * gradient
    first_hat = moment_one * (1.0 / (1.0 - BETA_ONE**step_num))
    second_hat = moment_two * (1.0 / (1.0 - BETA_TWO**step_num))
    master = master - LEARN_RATE * (
        first_hat / (jnp.sqrt(second_hat) + ADAM_EPS) + DECAY_RATE * master
    )
    return (master, moment_one, moment_two)


class Sems:
    def __init__(self, send, recv):
        self.send, self.recv, self.index = send, recv, {}

    def pair(self, *name):
        slot = self.index.setdefault(name, len(self.index))
        return self.send.at[slot], self.recv.at[slot]


N_SEMS = 400
RELAY_BY = (1, 3, 1, 3)
N_SUMS = 19
HOPS = (2, 2)


def sums_of(parts, hops):
    (_, a), (_, b), (_, d) = parts
    height = a + b + d
    return [
        (2, 4, height, VW), (4, 4, height, VW), (2, 2, a, VW),
        (2, 4, a, VW), (3, 4, 4, b, LANES), (3, 4, d, VW),
        (4, a, VW), (4, 4, b, LANES), (4, d, VW),
        (4, a, VW) if hops == 2 else (4, 4, a, LANES), (4, 4, b, LANES), (4, 4, d, LANES),
        (a, VW), (4, b, LANES), (4, d, LANES),
        (4, a, LANES), (4, b, LANES), (4, d, LANES),
        (height, LANES),
    ]


def f32(value):
    return value.astype(jnp.float32)


def kernel(
    states_hbm, read_hbm, shift_ref, adv_ref, mask_ref, len_ref, slot_ref, w_hbm, m_hbm, v_hbm,
    out_ref,
    st, st_t, rd, meta, w_ref, m_ref, v_ref, wh, acc, sc, cnt, cnt_in,
    load_sem, send_sem, recv_sem, *sums,
):
    dp, sh = lax.axis_index("dp"), lax.axis_index("shard")
    xl, z = dp // 4, dp % 4
    y, xh, c = sh // 4, (sh // 2) % 2, sh % 2
    x = xh * 2 + xl

    def device(x_, y_, z_, c_):
        return ((x_ % 2) * 4 + z_, y_ * 4 + (x_ // 2) * 2 + c_)

    def turn(axis, d):
        return ({"x": x, "y": y, "z": z}[axis] + d) % 4

    def peer(axis, d):
        to = turn(axis, d)
        return device(
            to if axis == "x" else x, to if axis == "y" else y, to if axis == "z" else z, c
        )

    twin = device(x, y, z, 1 - c)
    pair = xh * 2 + (1 - xl)
    replicas = [device(pair, y, turn("z", d), c) for d in range(4)]
    across_xy = [device(turn("x", 2), turn("y", d), z, c) for d in range(4)]
    flip = (x, pair, turn("x", 2), 3 - x)
    flipped = [device(to, y, z, c) for to in flip]

    def lanes(index):
        return pl.ds(pl.multiple_of(index * LANES, LANES), LANES)

    zc = lanes(z)
    sems = Sems(send_sem, recv_sem)

    def send(src, dst, to, *name):
        send_at, recv_at = sems.pair(*name)
        copy = pltpu.make_async_remote_copy(
            src_ref=src, dst_ref=dst, send_sem=send_at, recv_sem=recv_at,
            device_id=to, device_id_type=MESH,
        )
        copy.start()
        return copy

    own_rows = pl.ds(pl.multiple_of(xl * PIECE, PIECE), PIECE)

    loads = [pltpu.make_async_copy(w_hbm, w_ref, load_sem.at[0])]
    for k in range(4):
        cols = pl.ds(k * 1280, 1280)
        loads.append(
            pltpu.make_async_copy(states_hbm.at[:, cols], st.at[:, cols], load_sem.at[1 + k])
        )
    loads.append(pltpu.make_async_copy(read_hbm, rd, load_sem.at[5]))
    loads.append(pltpu.make_async_copy(m_hbm.at[own_rows, zc], m_ref, load_sem.at[6]))
    loads.append(pltpu.make_async_copy(v_hbm.at[own_rows, zc], v_ref, load_sem.at[7]))
    for load in loads:
        load.start()

    barrier = pltpu.get_barrier_semaphore()
    greeted = [peer(axis, d) for axis in "xyz" for d in (1, 2, 3)] + [twin]
    greeted += across_xy[1:]
    for to in greeted:
        pl.semaphore_signal(barrier, inc=1, device_id=to, device_id_type=MESH)

    loads[0].wait()
    for half in range(2):
        for (first, size), cols in zip(WHOLE, (slice(None), zc, slice(None))):
            rows = pl.ds(half * PIECE + first, size)
            wh[c, y, 2 * xh + half, pl.ds(first, size), cols] = w_ref[rows, cols].astype(
                jnp.bfloat16
            )
    pl.semaphore_wait(barrier, len(greeted))

    def prepare():
        def line(ref):
            row = f32(ref[...]).reshape(1, ROWS)
            return jnp.concatenate([row, jnp.zeros((1, KPAD - ROWS), jnp.float32)], axis=1)

        slot = line(slot_ref)
        place = lax.broadcasted_iota(jnp.int32, (1, KPAD), 1)
        live = (place < len_ref[0]) & (slot >= 0.0) & (place < ROWS)
        batch = jnp.floor((slot + 0.5) * (1.0 / MB))
        odd = batch - 2.0 * jnp.floor(batch * 0.5)
        token = jnp.where(live, line(mask_ref), 0.0)
        tokens = [jnp.where(odd < 0.5, token, 0.0), jnp.where(odd < 0.5, 0.0, token)]
        lines = [line(shift_ref), line(adv_ref)] + tokens
        meta[...] = jnp.concatenate(lines + [jnp.zeros((4, KPAD), jnp.float32)], axis=0).T
        lane = lax.broadcasted_iota(jnp.int32, (8, LANES), 1)
        sums_now = [jnp.sum(row, axis=1, keepdims=True) for row in tokens]
        cnt[...] = jnp.where(lane == 0, sums_now[0], jnp.where(lane == 1, sums_now[1], 0.0))
        sc[pl.ds(ROWS, KPAD - ROWS), :] = jnp.zeros((KPAD - ROWS, VW), jnp.bfloat16)

    def count_start(stage, axis):
        return [
            send(cnt, cnt_in.at[stage, d - 1], peer(axis, d), "cnt", stage, d) for d in (1, 2, 3)
        ]

    def count_end(stage, copies):
        for copy in copies:
            copy.wait()
        total = cnt[...]
        for d in range(3):
            total = total + cnt_in[stage, d]
        cnt[...] = total

    def transpose_chunk(k):
        loads[1 + k].wait()

        def step(j, carry):
            cols = pl.ds(pl.multiple_of(k * 1280 + j * LANES, LANES), LANES)
            block = jnp.concatenate(
                [st[:, cols], jnp.zeros((KPAD - ROWS, LANES), jnp.bfloat16)], axis=0
            )
            st_t[cols, :] = block.T
            return carry

        lax.fori_loop(0, 10, step, 0)

    def fwd_chunk(yy, first):
        def step(i, carry):
            rows = pl.ds(pl.multiple_of(i * ROW_TILE, ROW_TILE), ROW_TILE)
            weight = jnp.concatenate(
                [
                    wh[core, yy, pl.ds(2 * half, 2)].reshape(2 * PIECE, VW)
                    for half in (0, 1)
                    for core in (0, 1)
                ],
                axis=0,
            )
            cols = pl.ds(pl.multiple_of(yy * 1280, 1280), 1280)
            proj = jnp.dot(st[rows, cols], weight, preferred_element_type=jnp.float32)
            prod = proj * f32(rd[rows, :])
            part = (
                prod[:, 0:128] + prod[:, 128:256] + prod[:, 256:384] + prod[:, 384:512]
            )
            if first:
                acc[rows, :] = part
            else:
                acc[rows, :] += part
            return carry

        lax.fori_loop(0, ROWS // ROW_TILE, step, 0)

    def scale_rows(u):
        total = jnp.maximum(cnt[0:1, u : u + 1], 1.0)

        def step(i, carry):
            rows = pl.ds(pl.multiple_of(i * ROW_TILE, ROW_TILE), ROW_TILE)
            shift, adv = meta[rows, 0:1], meta[rows, 1:2]
            weights = meta[rows, 2 + u : 3 + u]
            log_ratio = shift + jnp.sum(acc[rows, :], axis=1, keepdims=True)
            ratio = jnp.exp(log_ratio)
            clipped = jnp.clip(ratio, 1.0 - CLIP_EPS, 1.0 + CLIP_EPS)
            chosen = ratio * adv <= clipped * adv
            coeff = jnp.where(
                (weights > 0.0) & chosen, -(weights / total) * adv * ratio, 0.0
            )
            sc[rows, :] = (coeff * f32(rd[rows, :])).astype(jnp.bfloat16)
            return carry

        lax.fori_loop(0, ROWS // ROW_TILE, step, 0)

    def grad_block(core, yy, halves, first, height):
        blocks = []
        for half in halves:
            for low in (0, 1):
                start = yy * 1280 + half * 640 + core * 320 + low * PIECE + first
                blocks.append(st_t[pl.ds(pl.multiple_of(start, 16), height), :])
        product = jnp.dot(
            jnp.concatenate(blocks, axis=0), sc[...], preferred_element_type=jnp.float32
        )
        return product.reshape(len(blocks), height, VW)

    def add_up(own, parts):
        total = f32(own)
        for part in parts:
            total = total + f32(part)
        return total

    def share(u, p):
        first, size = WHOLE[p]
        block = out_ref.at[u, pl.ds(pl.multiple_of(xl * PIECE + first, 16), size), zc]
        return [send(block, block, replicas[d], "share", u, p, 1, d) for d in range(4)] + [
            send(block, block, peer("z", d), "share", u, p, 0, d) for d in (2, 1, 3)
        ]

    class Gather:
        def __init__(self, name, parts):
            self.name = name
            self.rows = [pl.ds(first, size) for first, size in parts]
            self.sent, self.part_y, self.part_z, self.part_x = [], {}, {}, {}
            self.relays, self.first = [], {}

        def ring(self, axis, block, *name, to=(1, 3, 2)):
            copies = {}
            for d in to:
                target = flipped[d] if axis == "x" else peer(axis, d)
                copies[d] = send(block, block, target, self.name, *name, d)
            self.sent.extend(copies.values())
            return copies

        def begin(self, p):
            block = wh.at[c, y, x, self.rows[p], zc]
            self.first[p] = self.ring("zxy"[p], block, "ag1", p)

        def along_y(self, g):
            block = wh.at[c, y, flip[g], self.rows[0], :]
            self.part_y[g] = self.ring("y", block, "y", g, to=(1, 3))

        def along_z(self, o):
            block = wh.at[c, turn("y", o), :, self.rows[1], zc]
            self.part_z[o] = self.ring("z", block, "z", o)

        def along_x(self, o, to=(1, 3, 2)):
            block = wh.at[c, turn("y", o), x, self.rows[2], :]
            self.part_x[o] = self.ring("x", block, "x", o, to=to)

        def relay(self, *blocks):
            for g in blocks:
                d = RELAY_BY[g]
                self.part_y[g][d].wait_recv()
                block = wh.at[c, turn("y", -d), flip[g], self.rows[0], :]
                self.relays.append(send(block, block, peer("y", d), self.name, "relay", g))

        def arrived(self, o):
            if o == 2:
                for copy in self.relays:
                    copy.wait_recv()
            elif o:
                for g in range(4):
                    if RELAY_BY[g] != 4 - o:
                        self.part_y[g][4 - o].wait_recv()
            for copy in list(self.part_z[o].values()) + list(self.part_x[o].values()):
                copy.wait_recv()

    def gather_first(gather):
        second = gather.ring("x", wh.at[c, y, x, gather.rows[0], :], "ag2", 0, to=(3, 2))
        both = wh.at[c, y, pl.ds(2 * xh, 2), gather.rows[1], zc]
        plane = [send(both, both, across_xy[0], "ag2", 1, 0)]
        plane += [send(both, both, peer("y", d), "ag2", 1, 1, d) for d in (1, 2, 3)]
        plane += [send(both, both, across_xy[d], "ag2", 1, 2, d) for d in (1, 2, 3)]
        gather.sent += plane
        third = gather.ring("y", wh.at[c, y, x, gather.rows[2], :], "ag2", 2)
        gather.along_x(0, to=(3, 2))
        gather.along_y(0)
        gather.along_y(1)
        prepare()
        counting = count_start(0, "z")
        transpose_chunk(0)
        count_end(0, counting)
        counting = count_start(1, "x")
        for copy in plane:
            copy.wait_recv()
        gather.along_z(0)
        for g in (3, 2):
            second[g].wait_recv()
            gather.along_y(g)
        for o in (1, 3, 2):
            gather.along_z(o)
            third[4 - o].wait_recv()
            gather.along_x(o)

        def between():
            gather.relay(0, 1)
            transpose_chunk(1)
            count_end(1, counting)
            counting_y = count_start(2, "y")
            gather.relay(2, 3)
            transpose_chunk(2)
            transpose_chunk(3)
            count_end(2, counting_y)
            loads[5].wait()

        return between

    def gather_steps(gather):
        first = gather.first
        for copy in first[0].values():
            copy.wait_recv()
        second = [gather.ring("x", wh.at[c, y, x, gather.rows[0], :], "ag2", 0)]
        for copy in first[1].values():
            copy.wait_recv()
        second.append(gather.ring("y", wh.at[c, y, :, gather.rows[1], zc], "ag2", 1))
        for copy in first[2].values():
            copy.wait_recv()
        second.append(gather.ring("z", wh.at[c, :, x, gather.rows[2], zc], "ag2", 2))
        gather.along_y(0)
        gather.along_z(0)
        yield
        for g in (1, 3):
            second[0][g].wait_recv()
            gather.along_y(g)
        for copy in second[2].values():
            copy.wait_recv()
        gather.along_x(0)
        second[0][2].wait_recv()
        gather.along_y(2)
        for o in (1, 3, 2):
            second[1][4 - o].wait_recv()
            gather.along_z(o)
            gather.along_x(o)
        yield
        gather.relay(0, 1)

    def reduce_steps(u, h, given, sent, done):
        kind, parts = SUM_TYPES[u], STREAMS[u][h]
        base, height = parts[0][0], sum(size for _, size in parts)
        rows = [pl.ds(first - base, size) for first, size in parts]
        at = N_SUMS * (h if u == 0 else len(STREAMS[0]))
        gsend, gs, rel, r0, r1, r2, s0, s1, s2, q0, q1, q2, *rest, total = sums[at : at + N_SUMS]
        t0, t1, t2, e0, e1, e2 = rest
        outs, relayed, hop = {}, [], {0: [], 1: [], 2: []}

        def give(i):
            yy = turn("y", CHUNKS_OUT[i])
            if i >= 2:
                for copy in given[-2]:
                    copy.wait_send()
            gift = []
            for k in (0, 1):
                these = pl.ds(2 * k, 2)
                gsend[i % 2, these] = grad_block(1 - c, yy, (k,), base, height).astype(kind)
                gift.append(
                    send(gsend.at[i % 2, these], gs.at[yy, these], twin, "rsc", h, i, k)
                )
            given.append(gift)
            return gift

        def keep(i):
            yy = turn("y", CHUNKS_OUT[i])
            for k in (0, 1):
                these = pl.ds(2 * k, 2)
                gifts[i][k].wait_recv()
                gs[yy, these] = (
                    grad_block(c, yy, (k,), base, height) + f32(gs[yy, these])
                ).astype(kind)

        def first_sends(o):
            yy = turn("y", o)
            for d in (2, 1, 3):
                outs[1, o, d] = send(
                    gs.at[yy, :, rows[1], lanes(turn("z", d))], r1.at[d - 1, yy],
                    peer("z", d), "rs1", h, 1, o, d,
                )
                outs[2, o, d] = send(
                    gs.at[yy, turn("x", d), rows[2], :], r2.at[d - 1, yy],
                    peer("x", d), "rs1", h, 2, o, d,
                )

        def first_sums(o):
            yy = turn("y", o)
            for d in (1, 2, 3):
                outs[1, o, d].wait_recv()
            s1[yy] = add_up(gs[yy, :, rows[1], zc], [r1[d, yy] for d in range(3)]).astype(kind)
            if HOPS[u] == 2 and o:
                hop[1].append(send(s1.at[yy], q1.at[o], peer("y", o), "rs2", h, 1, o))
            for d in (2, 1, 3, 0):
                if HOPS[u] == 1 and (o or d):
                    xx = turn("x", d)
                    hop[1].append(
                        send(
                            s1.at[yy, xx], q1.at[o, d], device(xx, yy, z, c),
                            "rs2", h, 1, o, d,
                        )
                    )
            for d in (1, 2, 3):
                outs[2, o, d].wait_recv()
            s2[yy] = add_up(gs[yy, x, rows[2], :], [r2[d, yy] for d in range(3)]).astype(kind)
            for d in (2, 1, 3, 0):
                if HOPS[u] == 2 and d:
                    hop[2].append(
                        send(
                            s2.at[yy, :, lanes(turn("z", d))], q2.at[d, yy], peer("z", d),
                            "rs2", h, 2, o, d,
                        )
                    )
                elif HOPS[u] == 1 and (o or d):
                    zz = turn("z", d)
                    hop[2].append(
                        send(
                            s2.at[yy, :, lanes(zz)], q2.at[o, d], device(x, yy, zz, c),
                            "rs2", h, 2, o, d,
                        )
                    )

        def pass_on(o):
            yy = turn("y", o)
            side = 0 if o == 1 else 1
            relayed[side].wait_recv()
            for k in range(2):
                gs[yy, 2 * side + k, rows[0], :] = (
                    f32(gs[yy, 2 * side + k, rows[0], :]) + f32(rel[side, k])
                ).astype(kind)
            outs[0, o, 0] = send(
                gs.at[yy, :, rows[0], :], r0.at[side], peer("y", o), "rs1", h, 0, o
            )

        gifts = [give(0)]
        for i, o in enumerate(CHUNKS_OUT):
            if i + 1 < 4:
                gifts.append(give(i + 1))
            keep(i)
            if i == 0:
                relayed += [
                    send(
                        gs.at[turn("y", 2), pl.ds(2 * side, 2), rows[0], :], rel.at[side],
                        peer("y", 1 + 2 * side), "rs0", h, side,
                    )
                    for side in range(2)
                ]
            first_sends(o)
            if i == 2:
                pass_on(CHUNKS_OUT[1])
                pass_on(CHUNKS_OUT[2])
            yield
        first_sums(CHUNKS_OUT[0])
        first_sums(CHUNKS_OUT[1])
        yield
        for o in (1, 3):
            outs[0, o, 0].wait_recv()
        for d in (2, 1, 3, 0):
            xx = turn("x", d)
            s0[xx] = add_up(gs[y, xx, rows[0], :], [r0[0, xx], r0[1, xx]]).astype(kind)
            if HOPS[u] == 2 and d:
                hop[0].append(send(s0.at[xx], q0.at[d], peer("x", d), "rs2", h, 0, d))
            for e in (2, 1, 3, 0):
                if HOPS[u] == 1 and (d or e):
                    zz = turn("z", e)
                    hop[0].append(
                        send(
                            s0.at[xx, :, lanes(zz)], q0.at[d, e], device(xx, y, zz, c),
                            "rs2", h, 0, d, e,
                        )
                    )
        first_sums(CHUNKS_OUT[2])
        first_sums(CHUNKS_OUT[3])
        yield
        others = [(d, e) for d in range(4) for e in range(4) if d or e]
        if u == 0 and h == 0:
            for load in loads[6:]:
                load.wait()
        last = {}
        if HOPS[u] == 2:
            for p in (1, 2, 0):
                for copy in hop[p]:
                    copy.wait_recv()
                if p == 0:
                    t0[...] = add_up(s0[x], [q0[d] for d in (1, 2, 3)]).astype(kind)
                elif p == 1:
                    t1[...] = add_up(s1[y], [q1[d] for d in (1, 2, 3)]).astype(kind)
                else:
                    t2[...] = add_up(s2[:, :, zc], [q2[d] for d in (1, 2, 3)]).astype(kind)
                last[p] = []
                for d in (2, 1, 3):
                    axis = "zxy"[p]
                    block = (
                        t0.at[:, lanes(turn("z", d))], t1.at[turn("x", d)], t2.at[turn("y", d)]
                    )[p]
                    last[p].append(
                        send(block, (e0, e1, e2)[p].at[d], peer(axis, d), "rs3", h, p, d)
                    )
        for p in (1, 2, 0):
            if HOPS[u] == 2:
                for copy in last[p]:
                    copy.wait_recv()
                hop[p] += last[p]
                own = (lambda: t0[:, zc], lambda: t1[x], lambda: t2[y])[p]()
                got = [(e0, e1, e2)[p][d] for d in (1, 2, 3)]
            else:
                for copy in hop[p]:
                    copy.wait_recv()
                own = (lambda: s0[x, :, zc], lambda: s1[y, x], lambda: s2[y, :, zc])[p]()
                got = [(q0, q1, q2)[p][d, e] for d, e in others]
            total[rows[p], :] = add_up(own, got)
            gradient = total[rows[p], :]
            first, size = parts[p]
            mine = pl.ds(pl.multiple_of(xl * PIECE + first, 16), size)
            out_ref[u, mine, zc] = gradient.astype(jnp.bfloat16)
            if u == 0:
                these = pl.ds(first, size)
                master, _, _ = adam_step(
                    w_ref[mine, zc], m_ref[these, :], v_ref[these, :], gradient, PRIOR_STEPS + 1
                )
                wh[c, y, x, these, zc] = master.astype(jnp.bfloat16)
            done(p)
        sent += relayed + [copy for gift in gifts[2:] for copy in gift]
        sent += list(outs.values()) + hop[0] + hop[1] + hop[2]

    def stream_steps(h, gather, given, sent):
        yield from reduce_steps(0, h, given, sent, gather.begin)
        yield from gather_steps(gather)

    def multiply(gathers, between, before_last):
        across = {}

        def cross(o):
            for gather in gathers:
                gather.arrived(o)
            block = wh.at[c, turn("y", o)]
            across[o] = send(block, block, twin, "agc", o)

        cross(CHUNKS_IN[0])
        between()
        for i, o in enumerate(CHUNKS_IN):
            if i < 3:
                cross(CHUNKS_IN[i + 1])
            if i == 2:
                before_last()
            across[o].wait_recv()
            fwd_chunk(turn("y", o), i == 0)
        return list(across.values()) + [copy for gather in gathers for copy in gather.sent + gather.relays]

    shared, counting = [], []
    gathers = [Gather("w0", WHOLE)]
    between = gather_first(gathers[0])
    sent = multiply(
        gathers, between, lambda: counting.append(send(cnt, cnt_in.at[3, 0], twin, "cnt", 3))
    )
    counting[0].wait()
    cnt[...] = cnt[...] + cnt_in[3, 0]
    scale_rows(0)
    for copy in sent:
        copy.wait_send()

    sent, given = [], []
    gathers = [Gather("w1" + "ab"[h], parts) for h, parts in enumerate(STREAMS[0])]
    running = [stream_steps(h, gathers[h], given, sent) for h in range(len(gathers))]
    for _ in range(4):
        next(running[0])
    running = running[::-1]
    while running:
        running = [steps for steps in running if next(steps, running) is not running]
    sent += multiply(
        gathers,
        lambda: [gather.relay(2, 3) for gather in gathers],
        lambda: shared.extend(copy for p in range(3) for copy in share(0, p)),
    )
    scale_rows(1)
    for copy in sent:
        copy.wait_send()

    sent = []
    for _ in reduce_steps(1, 0, [], sent, lambda p: shared.extend(share(1, p))):
        pass
    for copy in shared:
        copy.wait_recv()
    for copy in sent + shared:
        copy.wait_send()


def body(
    states, readout, logp_shift, advantage, response_mask, rollout_len, dest_slot,
    weight, moment1, moment2,
):
    bf16, full = jnp.bfloat16, jnp.float32
    vmem = pl.BlockSpec(memory_space=pltpu.VMEM)
    hbm = pl.BlockSpec(memory_space=pl.ANY)
    smem = pl.BlockSpec(memory_space=pltpu.SMEM)
    sums = []
    for kind, hops, streams in zip(SUM_TYPES, HOPS, STREAMS):
        for parts in streams:
            *parcels, total = sums_of(parts, hops)
            sums += [pltpu.VMEM(dims, kind) for dims in parcels] + [pltpu.VMEM(total, full)]
    gradients = pl.pallas_call(
        kernel,
        out_shape=jax.ShapeDtypeStruct((UPDATES,) + weight.shape, bf16),
        in_specs=[hbm, hbm, vmem, vmem, vmem, smem, vmem, hbm, hbm, hbm],
        out_specs=vmem,
        scratch_shapes=[
            pltpu.VMEM((ROWS, D), bf16),
            pltpu.VMEM((D, KPAD), bf16),
            pltpu.VMEM((ROWS, VW), bf16),
            pltpu.VMEM((KPAD, 8), full),
            pltpu.VMEM((2 * PIECE, VW), full),
            pltpu.VMEM((PIECE, LANES), full),
            pltpu.VMEM((PIECE, LANES), full),
            pltpu.VMEM((2, 4, 4, PIECE, VW), bf16),
            pltpu.VMEM((ROWS, LANES), full),
            pltpu.VMEM((KPAD, VW), bf16),
            pltpu.VMEM((8, LANES), full),
            pltpu.VMEM((4, 3, 8, LANES), full),
            pltpu.SemaphoreType.DMA((8,)),
            pltpu.SemaphoreType.DMA((N_SEMS,)),
            pltpu.SemaphoreType.DMA((N_SEMS,)),
        ]
        + sums,
        compiler_params=pltpu.CompilerParams(
            collective_id=0, has_side_effects=True, vmem_limit_bytes=58 * 1024 * 1024
        ),
    )(
        states, readout, logp_shift, advantage, response_mask, rollout_len, dest_slot,
        weight, moment1, moment2,
    )
    master, one, two = weight, moment1, moment2
    for u in range(UPDATES):
        master, one, two = adam_step(
            master, one, two, gradients[u].astype(full), PRIOR_STEPS + u + 1
        )
    return master, one, two


def solution(mesh):
    rows = P(("dp", "shard"))
    return jax.shard_map(
        body,
        mesh=mesh,
        in_specs=(
            P(("dp", "shard"), None), P(("dp", "shard"), None), rows, rows, rows, rows, rows,
            P("shard", None), P("shard", None), P("shard", None),
        ),
        out_specs=(P("shard", None), P("shard", None), P("shard", None)),
        check_vma=False,
    )
```

```python
import jax
import jax.numpy as jnp
from jax import lax
from jax.experimental import pallas as pl
from jax.experimental.pallas import tpu as pltpu
from jax.sharding import PartitionSpec as P

MESH = pl.DeviceIdType.MESH

BAL = 576
UPDATES = 2
PRIOR_STEPS = 100
MB = 288
ROWS = 864
KPAD = 896
D = 5120
VW = 512
PIECE = 160
LANES = 128
ROW_TILE = 864

BETA_ONE = 0.9
BETA_TWO = 0.999
LEARN_RATE = 0.001
DECAY_RATE = 0.01
ADAM_EPS = 1e-08
CLIP_EPS = 0.2

WHOLE = ((0, 64), (64, 48), (112, 48))
STREAMS = (
    (WHOLE,),
    (WHOLE,),
)
SUM_TYPES = (jnp.float32, jnp.bfloat16)
CHUNKS_IN = (0, 1, 3, 2)
CHUNKS_OUT = (2, 1, 3, 0)


def adam_step(master, moment_one, moment_two, gradient, step_num):
    moment_one = BETA_ONE * moment_one + (1.0 - BETA_ONE) * gradient
    moment_two = BETA_TWO * moment_two + (1.0 - BETA_TWO) * gradient * gradient
    first_hat = moment_one * (1.0 / (1.0 - BETA_ONE**step_num))
    second_hat = moment_two * (1.0 / (1.0 - BETA_TWO**step_num))
    master = master - LEARN_RATE * (
        first_hat / (jnp.sqrt(second_hat) + ADAM_EPS) + DECAY_RATE * master
    )
    return (master, moment_one, moment_two)


class Sems:
    def __init__(self, send, recv):
        self.send, self.recv, self.index = send, recv, {}

    def pair(self, *name):
        slot = self.index.setdefault(name, len(self.index))
        return self.send.at[slot], self.recv.at[slot]


N_SEMS = 400
RELAY_BY = (1, 3, 1, 3)
N_SUMS = 19
HOPS = (2, 2)


def sums_of(parts, hops):
    (_, a), (_, b), (_, d) = parts
    height = a + b + d
    return [
        (2, 4, height, VW), (4, 4, height, VW), (2, 2, a, VW),
        (2, 4, a, VW), (3, 4, 4, b, LANES), (3, 4, d, VW),
        (4, a, VW), (4, 4, b, LANES), (4, d, VW),
        (4, a, VW) if hops == 2 else (4, 4, a, LANES), (4, 4, b, LANES), (4, 4, d, LANES),
        (a, VW), (4, b, LANES), (4, d, LANES),
        (4, a, LANES), (4, b, LANES), (4, d, LANES),
        (height, LANES),
    ]


def f32(value):
    return value.astype(jnp.float32)


def kernel(
    states_hbm, read_hbm, shift_ref, adv_ref, mask_ref, len_ref, slot_ref, w_hbm, m_hbm, v_hbm,
    out_ref,
    st, st_t, rd, meta, w_ref, m_ref, v_ref, wh, acc, sc, cnt, cnt_in,
    load_sem, send_sem, recv_sem, *sums,
):
    dp, sh = lax.axis_index("dp"), lax.axis_index("shard")
    xl, z = dp // 4, dp % 4
    y, xh, c = sh // 4, (sh // 2) % 2, sh % 2
    x = xh * 2 + xl

    def device(x_, y_, z_, c_):
        return ((x_ % 2) * 4 + z_, y_ * 4 + (x_ // 2) * 2 + c_)

    def turn(axis, d):
        return ({"x": x, "y": y, "z": z}[axis] + d) % 4

    def peer(axis, d):
        to = turn(axis, d)
        return device(
            to if axis == "x" else x, to if axis == "y" else y, to if axis == "z" else z, c
        )

    twin = device(x, y, z, 1 - c)
    pair = xh * 2 + (1 - xl)
    replicas = [device(pair, y, turn("z", d), c) for d in range(4)]
    across_xy = [device(turn("x", 2), turn("y", d), z, c) for d in range(4)]
    flip = (x, pair, turn("x", 2), 3 - x)
    flipped = [device(to, y, z, c) for to in flip]

    def lanes(index):
        return pl.ds(pl.multiple_of(index * LANES, LANES), LANES)

    zc = lanes(z)
    sems = Sems(send_sem, recv_sem)

    def send(src, dst, to, *name):
        send_at, recv_at = sems.pair(*name)
        copy = pltpu.make_async_remote_copy(
            src_ref=src, dst_ref=dst, send_sem=send_at, recv_sem=recv_at,
            device_id=to, device_id_type=MESH,
        )
        copy.start()
        return copy

    own_rows = pl.ds(pl.multiple_of(xl * PIECE, PIECE), PIECE)

    loads = [pltpu.make_async_copy(w_hbm, w_ref, load_sem.at[0])]
    for k in range(4):
        cols = pl.ds(k * 1280, 1280)
        loads.append(
            pltpu.make_async_copy(states_hbm.at[:, cols], st.at[:, cols], load_sem.at[1 + k])
        )
    loads.append(pltpu.make_async_copy(read_hbm, rd, load_sem.at[5]))
    loads.append(pltpu.make_async_copy(m_hbm.at[own_rows, zc], m_ref, load_sem.at[6]))
    loads.append(pltpu.make_async_copy(v_hbm.at[own_rows, zc], v_ref, load_sem.at[7]))
    for load in loads:
        load.start()

    barrier = pltpu.get_barrier_semaphore()
    greeted = [peer(axis, d) for axis in "xyz" for d in (1, 2, 3)] + [twin]
    greeted += across_xy[1:]
    for to in greeted:
        pl.semaphore_signal(barrier, inc=1, device_id=to, device_id_type=MESH)

    loads[0].wait()
    for half in range(2):
        for (first, size), cols in zip(WHOLE, (slice(None), zc, slice(None))):
            rows = pl.ds(half * PIECE + first, size)
            wh[c, y, 2 * xh + half, pl.ds(first, size), cols] = w_ref[rows, cols].astype(
                jnp.bfloat16
            )
    pl.semaphore_wait(barrier, len(greeted))

    def prepare():
        def line(ref):
            row = f32(ref[...]).reshape(1, ROWS)
            return jnp.concatenate([row, jnp.zeros((1, KPAD - ROWS), jnp.float32)], axis=1)

        slot = line(slot_ref)
        place = lax.broadcasted_iota(jnp.int32, (1, KPAD), 1)
        live = (place < len_ref[0]) & (slot >= 0.0) & (place < ROWS)
        batch = jnp.floor((slot + 0.5) * (1.0 / MB))
        odd = batch - 2.0 * jnp.floor(batch * 0.5)
        token = jnp.where(live, line(mask_ref), 0.0)
        tokens = [jnp.where(odd < 0.5, token, 0.0), jnp.where(odd < 0.5, 0.0, token)]
        lines = [line(shift_ref), line(adv_ref)] + tokens
        meta[...] = jnp.concatenate(lines + [jnp.zeros((4, KPAD), jnp.float32)], axis=0).T
        lane = lax.broadcasted_iota(jnp.int32, (8, LANES), 1)
        sums_now = [jnp.sum(row, axis=1, keepdims=True) for row in tokens]
        cnt[...] = jnp.where(lane == 0, sums_now[0], jnp.where(lane == 1, sums_now[1], 0.0))
        sc[pl.ds(ROWS, KPAD - ROWS), :] = jnp.zeros((KPAD - ROWS, VW), jnp.bfloat16)

    def count_start(stage, axis):
        return [
            send(cnt, cnt_in.at[stage, d - 1], peer(axis, d), "cnt", stage, d) for d in (1, 2, 3)
        ]

    def count_end(stage, copies):
        for copy in copies:
            copy.wait()
        total = cnt[...]
        for d in range(3):
            total = total + cnt_in[stage, d]
        cnt[...] = total

    def transpose_chunk(k):
        loads[1 + k].wait()

        def step(j, carry):
            cols = pl.ds(pl.multiple_of(k * 1280 + j * LANES, LANES), LANES)
            block = jnp.concatenate(
                [st[:, cols], jnp.zeros((KPAD - ROWS, LANES), jnp.bfloat16)], axis=0
            )
            st_t[cols, :] = block.T
            return carry

        lax.fori_loop(0, 10, step, 0)

    def fwd_chunk(yy, first):
        def step(i, carry):
            rows = pl.ds(pl.multiple_of(i * ROW_TILE, ROW_TILE), ROW_TILE)
            weight = jnp.concatenate(
                [
                    wh[core, yy, pl.ds(2 * half, 2)].reshape(2 * PIECE, VW)
                    for half in (0, 1)
                    for core in (0, 1)
                ],
                axis=0,
            )
            cols = pl.ds(pl.multiple_of(yy * 1280, 1280), 1280)
            proj = jnp.dot(st[rows, cols], weight, preferred_element_type=jnp.float32)
            prod = proj * f32(rd[rows, :])
            part = (
                prod[:, 0:128] + prod[:, 128:256] + prod[:, 256:384] + prod[:, 384:512]
            )
            if first:
                acc[rows, :] = part
            else:
                acc[rows, :] += part
            return carry

        lax.fori_loop(0, ROWS // ROW_TILE, step, 0)

    def scale_rows(u):
        total = jnp.maximum(cnt[0:1, u : u + 1], 1.0)

        def step(i, carry):
            rows = pl.ds(pl.multiple_of(i * ROW_TILE, ROW_TILE), ROW_TILE)
            shift, adv = meta[rows, 0:1], meta[rows, 1:2]
            weights = meta[rows, 2 + u : 3 + u]
            log_ratio = shift + jnp.sum(acc[rows, :], axis=1, keepdims=True)
            ratio = jnp.exp(log_ratio)
            clipped = jnp.clip(ratio, 1.0 - CLIP_EPS, 1.0 + CLIP_EPS)
            chosen = ratio * adv <= clipped * adv
            coeff = jnp.where(
                (weights > 0.0) & chosen, -(weights / total) * adv * ratio, 0.0
            )
            sc[rows, :] = (coeff * f32(rd[rows, :])).astype(jnp.bfloat16)
            return carry

        lax.fori_loop(0, ROWS // ROW_TILE, step, 0)

    def grad_block(core, yy, halves, first, height):
        blocks = []
        for half in halves:
            for low in (0, 1):
                start = yy * 1280 + half * 640 + core * 320 + low * PIECE + first
                blocks.append(st_t[pl.ds(pl.multiple_of(start, 16), height), :])
        product = jnp.dot(
            jnp.concatenate(blocks, axis=0), sc[...], preferred_element_type=jnp.float32
        )
        return product.reshape(len(blocks), height, VW)

    def add_up(own, parts):
        total = f32(own)
        for part in parts:
            total = total + f32(part)
        return total

    def share(u, p):
        first, size = WHOLE[p]
        block = out_ref.at[u, pl.ds(pl.multiple_of(xl * PIECE + first, 16), size), zc]
        return [send(block, block, replicas[d], "share", u, p, 1, d) for d in range(4)] + [
            send(block, block, peer("z", d), "share", u, p, 0, d) for d in (2, 1, 3)
        ]

    class Gather:
        def __init__(self, name, parts):
            self.name = name
            self.rows = [pl.ds(first, size) for first, size in parts]
            self.sent, self.part_y, self.part_z, self.part_x = [], {}, {}, {}
            self.relays, self.first = [], {}

        def ring(self, axis, block, *name, to=(1, 3, 2)):
            copies = {}
            for d in to:
                target = flipped[d] if axis == "x" else peer(axis, d)
                copies[d] = send(block, block, target, self.name, *name, d)
            self.sent.extend(copies.values())
            return copies

        def begin(self, p):
            block = wh.at[c, y, x, self.rows[p], zc]
            self.first[p] = self.ring("zxy"[p], block, "ag1", p)

        def along_y(self, g):
            block = wh.at[c, y, flip[g], self.rows[0], :]
            self.part_y[g] = self.ring("y", block, "y", g, to=(1, 3))

        def along_z(self, o):
            block = wh.at[c, turn("y", o), :, self.rows[1], zc]
            self.part_z[o] = self.ring("z", block, "z", o)

        def along_x(self, o, to=(1, 3, 2)):
            block = wh.at[c, turn("y", o), x, self.rows[2], :]
            self.part_x[o] = self.ring("x", block, "x", o, to=to)

        def relay(self, *blocks):
            for g in blocks:
                d = RELAY_BY[g]
                self.part_y[g][d].wait_recv()
                block = wh.at[c, turn("y", -d), flip[g], self.rows[0], :]
                self.relays.append(send(block, block, peer("y", d), self.name, "relay", g))

        def arrived(self, o):
            if o == 2:
                for copy in self.relays:
                    copy.wait_recv()
            elif o:
                for g in range(4):
                    if RELAY_BY[g] != 4 - o:
                        self.part_y[g][4 - o].wait_recv()
            for copy in list(self.part_z[o].values()) + list(self.part_x[o].values()):
                copy.wait_recv()

    def gather_first(gather):
        second = gather.ring("x", wh.at[c, y, x, gather.rows[0], :], "ag2", 0, to=(3, 2))
        both = wh.at[c, y, pl.ds(2 * xh, 2), gather.rows[1], zc]
        plane = [send(both, both, across_xy[0], "ag2", 1, 0)]
        plane += [send(both, both, peer("y", d), "ag2", 1, 1, d) for d in (1, 2, 3)]
        plane += [send(both, both, across_xy[d], "ag2", 1, 2, d) for d in (1, 2, 3)]
        gather.sent += plane
        third = gather.ring("y", wh.at[c, y, x, gather.rows[2], :], "ag2", 2)
        gather.along_x(0, to=(3, 2))
        gather.along_y(0)
        gather.along_y(1)
        prepare()
        counting = count_start(0, "z")
        transpose_chunk(0)
        count_end(0, counting)
        counting = count_start(1, "x")
        for copy in plane:
            copy.wait_recv()
        gather.along_z(0)
        for g in (3, 2):
            second[g].wait_recv()
            gather.along_y(g)
        for o in (1, 3, 2):
            gather.along_z(o)
            third[4 - o].wait_recv()
            gather.along_x(o)

        def between():
            gather.relay(0, 1)
            transpose_chunk(1)
            count_end(1, counting)
            counting_y = count_start(2, "y")
            gather.relay(2, 3)
            transpose_chunk(2)
            transpose_chunk(3)
            count_end(2, counting_y)
            loads[5].wait()

        return between

    def gather_steps(gather):
        first = gather.first
        for copy in first[0].values():
            copy.wait_recv()
        second = [gather.ring("x", wh.at[c, y, x, gather.rows[0], :], "ag2", 0)]
        for copy in first[1].values():
            copy.wait_recv()
        second.append(gather.ring("y", wh.at[c, y, :, gather.rows[1], zc], "ag2", 1))
        for copy in first[2].values():
            copy.wait_recv()
        second.append(gather.ring("z", wh.at[c, :, x, gather.rows[2], zc], "ag2", 2))
        gather.along_y(0)
        gather.along_z(0)
        yield
        for g in (1, 3):
            second[0][g].wait_recv()
            gather.along_y(g)
        for copy in second[2].values():
            copy.wait_recv()
        gather.along_x(0)
        second[0][2].wait_recv()
        gather.along_y(2)
        for o in (1, 3, 2):
            second[1][4 - o].wait_recv()
            gather.along_z(o)
            gather.along_x(o)
        yield
        gather.relay(0, 1)

    def reduce_steps(u, h, given, sent, done):
        kind, parts = SUM_TYPES[u], STREAMS[u][h]
        base, height = parts[0][0], sum(size for _, size in parts)
        rows = [pl.ds(first - base, size) for first, size in parts]
        at = N_SUMS * (h if u == 0 else len(STREAMS[0]))
        gsend, gs, rel, r0, r1, r2, s0, s1, s2, q0, q1, q2, *rest, total = sums[at : at + N_SUMS]
        t0, t1, t2, e0, e1, e2 = rest
        outs, relayed, hop = {}, [], {0: [], 1: [], 2: []}

        def give(i):
            yy = turn("y", CHUNKS_OUT[i])
            if i >= 2:
                for copy in given[-2]:
                    copy.wait_send()
            gift = []
            for k in (0, 1):
                these = pl.ds(2 * k, 2)
                gsend[i % 2, these] = grad_block(1 - c, yy, (k,), base, height).astype(kind)
                gift.append(
                    send(gsend.at[i % 2, these], gs.at[yy, these], twin, "rsc", h, i, k)
                )
            given.append(gift)
            return gift

        def keep(i):
            yy = turn("y", CHUNKS_OUT[i])
            for k in (0, 1):
                these = pl.ds(2 * k, 2)
                gifts[i][k].wait_recv()
                gs[yy, these] = (
                    grad_block(c, yy, (k,), base, height) + f32(gs[yy, these])
                ).astype(kind)

        def first_sends(o):
            yy = turn("y", o)
            for d in (2, 1, 3):
                outs[1, o, d] = send(
                    gs.at[yy, :, rows[1], lanes(turn("z", d))], r1.at[d - 1, yy],
                    peer("z", d), "rs1", h, 1, o, d,
                )
                outs[2, o, d] = send(
                    gs.at[yy, turn("x", d), rows[2], :], r2.at[d - 1, yy],
                    peer("x", d), "rs1", h, 2, o, d,
                )

        def first_sums(o):
            yy = turn("y", o)
            for d in (1, 2, 3):
                outs[1, o, d].wait_recv()
            s1[yy] = add_up(gs[yy, :, rows[1], zc], [r1[d, yy] for d in range(3)]).astype(kind)
            if HOPS[u] == 2 and o:
                hop[1].append(send(s1.at[yy], q1.at[o], peer("y", o), "rs2", h, 1, o))
            for d in (2, 1, 3, 0):
                if HOPS[u] == 1 and (o or d):
                    xx = turn("x", d)
                    hop[1].append(
                        send(
                            s1.at[yy, xx], q1.at[o, d], device(xx, yy, z, c),
                            "rs2", h, 1, o, d,
                        )
                    )
            for d in (1, 2, 3):
                outs[2, o, d].wait_recv()
            s2[yy] = add_up(gs[yy, x, rows[2], :], [r2[d, yy] for d in range(3)]).astype(kind)
            for d in (2, 1, 3, 0):
                if HOPS[u] == 2 and d:
                    hop[2].append(
                        send(
                            s2.at[yy, :, lanes(turn("z", d))], q2.at[d, yy], peer("z", d),
                            "rs2", h, 2, o, d,
                        )
                    )
                elif HOPS[u] == 1 and (o or d):
                    zz = turn("z", d)
                    hop[2].append(
                        send(
                            s2.at[yy, :, lanes(zz)], q2.at[o, d], device(x, yy, zz, c),
                            "rs2", h, 2, o, d,
                        )
                    )

        def pass_on(o):
            yy = turn("y", o)
            side = 0 if o == 1 else 1
            relayed[side].wait_recv()
            for k in range(2):
                gs[yy, 2 * side + k, rows[0], :] = (
                    f32(gs[yy, 2 * side + k, rows[0], :]) + f32(rel[side, k])
                ).astype(kind)
            outs[0, o, 0] = send(
                gs.at[yy, :, rows[0], :], r0.at[side], peer("y", o), "rs1", h, 0, o
            )

        gifts = [give(0)]
        for i, o in enumerate(CHUNKS_OUT):
            if i + 1 < 4:
                gifts.append(give(i + 1))
            keep(i)
            if i == 0:
                relayed += [
                    send(
                        gs.at[turn("y", 2), pl.ds(2 * side, 2), rows[0], :], rel.at[side],
                        peer("y", 1 + 2 * side), "rs0", h, side,
                    )
                    for side in range(2)
                ]
            first_sends(o)
            if i == 2:
                pass_on(CHUNKS_OUT[1])
                pass_on(CHUNKS_OUT[2])
            yield
        first_sums(CHUNKS_OUT[0])
        first_sums(CHUNKS_OUT[1])
        yield
        for o in (1, 3):
            outs[0, o, 0].wait_recv()
        for d in (2, 1, 3, 0):
            xx = turn("x", d)
            s0[xx] = add_up(gs[y, xx, rows[0], :], [r0[0, xx], r0[1, xx]]).astype(kind)
            if HOPS[u] == 2 and d:
                hop[0].append(send(s0.at[xx], q0.at[d], peer("x", d), "rs2", h, 0, d))
            for e in (2, 1, 3, 0):
                if HOPS[u] == 1 and (d or e):
                    zz = turn("z", e)
                    hop[0].append(
                        send(
                            s0.at[xx, :, lanes(zz)], q0.at[d, e], device(xx, y, zz, c),
                            "rs2", h, 0, d, e,
                        )
                    )
        first_sums(CHUNKS_OUT[2])
        first_sums(CHUNKS_OUT[3])
        yield
        others = [(d, e) for d in range(4) for e in range(4) if d or e]
        if u == 0 and h == 0:
            for load in loads[6:]:
                load.wait()
        last = {}
        if HOPS[u] == 2:
            for p in (1, 2, 0):
                for copy in hop[p]:
                    copy.wait_recv()
                if p == 0:
                    t0[...] = add_up(s0[x], [q0[d] for d in (1, 2, 3)]).astype(kind)
                elif p == 1:
                    t1[...] = add_up(s1[y], [q1[d] for d in (1, 2, 3)]).astype(kind)
                else:
                    t2[...] = add_up(s2[:, :, zc], [q2[d] for d in (1, 2, 3)]).astype(kind)
                last[p] = []
                for d in (2, 1, 3):
                    axis = "zxy"[p]
                    block = (
                        t0.at[:, lanes(turn("z", d))], t1.at[turn("x", d)], t2.at[turn("y", d)]
                    )[p]
                    last[p].append(
                        send(block, (e0, e1, e2)[p].at[d], peer(axis, d), "rs3", h, p, d)
                    )
        for p in (1, 2, 0):
            if HOPS[u] == 2:
                for copy in last[p]:
                    copy.wait_recv()
                hop[p] += last[p]
                own = (lambda: t0[:, zc], lambda: t1[x], lambda: t2[y])[p]()
                got = [(e0, e1, e2)[p][d] for d in (1, 2, 3)]
            else:
                for copy in hop[p]:
                    copy.wait_recv()
                own = (lambda: s0[x, :, zc], lambda: s1[y, x], lambda: s2[y, :, zc])[p]()
                got = [(q0, q1, q2)[p][d, e] for d, e in others]
            total[rows[p], :] = add_up(own, got)
            gradient = total[rows[p], :]
            first, size = parts[p]
            mine = pl.ds(pl.multiple_of(xl * PIECE + first, 16), size)
            out_ref[u, mine, zc] = gradient.astype(jnp.bfloat16)
            if u == 0:
                these = pl.ds(first, size)
                master, _, _ = adam_step(
                    w_ref[mine, zc], m_ref[these, :], v_ref[these, :], gradient, PRIOR_STEPS + 1
                )
                wh[c, y, x, these, zc] = master.astype(jnp.bfloat16)
            done(p)
        sent += relayed + [copy for gift in gifts[2:] for copy in gift]
        sent += list(outs.values()) + hop[0] + hop[1] + hop[2]

    def stream_steps(h, gather, given, sent):
        yield from reduce_steps(0, h, given, sent, gather.begin)
        yield from gather_steps(gather)

    def multiply(gathers, between, before_last):
        across = {}

        def cross(o):
            for gather in gathers:
                gather.arrived(o)
            block = wh.at[c, turn("y", o)]
            across[o] = send(block, block, twin, "agc", o)

        cross(CHUNKS_IN[0])
        between()
        for i, o in enumerate(CHUNKS_IN):
            if i < 3:
                cross(CHUNKS_IN[i + 1])
            if i == 2:
                before_last()
            across[o].wait_recv()
            fwd_chunk(turn("y", o), i == 0)
        return list(across.values()) + [copy for gather in gathers for copy in gather.sent + gather.relays]

    shared, counting = [], []
    gathers = [Gather("w0", WHOLE)]
    between = gather_first(gathers[0])
    sent = multiply(
        gathers, between, lambda: counting.append(send(cnt, cnt_in.at[3, 0], twin, "cnt", 3))
    )
    counting[0].wait()
    cnt[...] = cnt[...] + cnt_in[3, 0]
    scale_rows(0)
    for copy in sent:
        copy.wait_send()

    sent, given = [], []
    gathers = [Gather("w1" + "ab"[h], parts) for h, parts in enumerate(STREAMS[0])]
    running = [stream_steps(h, gathers[h], given, sent) for h in range(len(gathers))]
    for _ in range(4):
        next(running[0])
    running = running[::-1]
    while running:
        running = [steps for steps in running if next(steps, running) is not running]
    sent += multiply(
        gathers,
        lambda: [gather.relay(2, 3) for gather in gathers],
        lambda: shared.extend(copy for p in range(3) for copy in share(0, p)),
    )
    scale_rows(1)
    for copy in sent:
        copy.wait_send()

    sent = []
    for _ in reduce_steps(1, 0, [], sent, lambda p: shared.extend(share(1, p))):
        pass
    for copy in shared:
        copy.wait_recv()
    for copy in sent + shared:
        copy.wait_send()


def body(
    states, readout, logp_shift, advantage, response_mask, rollout_len, dest_slot,
    weight, moment1, moment2,
):
    bf16, full = jnp.bfloat16, jnp.float32
    vmem = pl.BlockSpec(memory_space=pltpu.VMEM)
    hbm = pl.BlockSpec(memory_space=pl.ANY)
    smem = pl.BlockSpec(memory_space=pltpu.SMEM)
    sums = []
    for kind, hops, streams in zip(SUM_TYPES, HOPS, STREAMS):
        for parts in streams:
            *parcels, total = sums_of(parts, hops)
            sums += [pltpu.VMEM(dims, kind) for dims in parcels] + [pltpu.VMEM(total, full)]
    gradients = pl.pallas_call(
        kernel,
        out_shape=jax.ShapeDtypeStruct((UPDATES,) + weight.shape, bf16),
        in_specs=[hbm, hbm, vmem, vmem, vmem, smem, vmem, hbm, hbm, hbm],
        out_specs=vmem,
        scratch_shapes=[
            pltpu.VMEM((ROWS, D), bf16),
            pltpu.VMEM((D, KPAD), bf16),
            pltpu.VMEM((ROWS, VW), bf16),
            pltpu.VMEM((KPAD, 8), full),
            pltpu.VMEM((2 * PIECE, VW), full),
            pltpu.VMEM((PIECE, LANES), full),
            pltpu.VMEM((PIECE, LANES), full),
            pltpu.VMEM((2, 4, 4, PIECE, VW), bf16),
            pltpu.VMEM((ROWS, LANES), full),
            pltpu.VMEM((KPAD, VW), bf16),
            pltpu.VMEM((8, LANES), full),
            pltpu.VMEM((4, 3, 8, LANES), full),
            pltpu.SemaphoreType.DMA((8,)),
            pltpu.SemaphoreType.DMA((N_SEMS,)),
            pltpu.SemaphoreType.DMA((N_SEMS,)),
        ]
        + sums,
        compiler_params=pltpu.CompilerParams(
            collective_id=0, has_side_effects=True, vmem_limit_bytes=58 * 1024 * 1024
        ),
    )(
        states, readout, logp_shift, advantage, response_mask, rollout_len, dest_slot,
        weight, moment1, moment2,
    )
    master, one, two = weight, moment1, moment2
    for u in range(UPDATES):
        master, one, two = adam_step(
            master, one, two, gradients[u].astype(full), PRIOR_STEPS + u + 1
        )
    return master, one, two


def solution(mesh):
    rows = P(("dp", "shard"))
    return jax.shard_map(
        body,
        mesh=mesh,
        in_specs=(
            P(("dp", "shard"), None), P(("dp", "shard"), None), rows, rows, rows, rows, rows,
            P("shard", None), P("shard", None), P("shard", None),
        ),
        out_specs=(P("shard", None), P("shard", None), P("shard", None)),
        check_vma=False,
    )
```
